256 devices in a mesh: section: 8 (over y, x_hi), dp: 32 (over z, x_lo, core).
Axes of the slice: x: 4 (x_hi: 2, x_lo: 2; x = x_hi * 2 + x_lo), y: 4, z: 8, core: 2. Of those that a mesh axis runs over, the one named last changes fastest.
Arguments:
- block_hidden_input: bfloat16 [4, 1024, 8192], P(None, 'dp'), may hold values from -6 to 6
- cached_score_gradient: float32 [4, 32], P(None, 'dp'), may hold values from -24 to 24
- value_projection: bfloat16 [8, 8192, 512], P('section', 'dp'), may hold values from -0.0625 to 0.0625
- output_projection: bfloat16 [8, 512, 8192], P('section', None, 'dp'), may hold values from -0.25 to 0.25
- adapter_down_factor: bfloat16 [8, 8192, 64], P('section', 'dp'), may hold values from -0.0625 to 0.0625
- adapter_up_factor: bfloat16 [8, 64, 512], P('section'), may hold values from -0.75 to 0.75
- input_norm_gain: float32 [8, 8192], P('section'), may hold values from 0.5 to 1.5
- last_norm_gain: float32 [8192], replicated, may hold values from 0.5 to 1.5
- scoring_head_weight: float32 [8192], replicated, may hold values from -0.0625 to 0.0625
Outputs:
- grad_down: float32 [8, 8192, 64], P('section', 'dp')
- grad_up: float32 [8, 64, 512], P('section')
The draws below stay inside these ranges and needn't reach their ends.
All inputs are finite; a program needn't handle non-finite values.
Results may differ from the reference program's by a relative error of at most 0.04.
Values may be sent and summed in bfloat16 or wider, within the bound.
A program may use at most 128 MiB of HBM per device.

```python
import jax
import jax.numpy as jnp
from jax import lax

MODEL_WIDTH = 8192
VALUE_WIDTH = 512
ADAPTER_RANK = 64
TOK_DEV = 32
MICRO = 4
CANDS = 32
TOKENS = 1024
N_SECTION = 8


def levels(stream_key, extent, cuts, low, top_value):
    factor_of = 1.0
    for axis_at, parts in cuts:
        heights = jax.random.uniform(jax.random.fold_in(jax.random.fold_in(stream_key, 6), axis_at), (parts,), jnp.float32, low / len(cuts), top_value / len(cuts))
        factor_of = factor_of * jnp.repeat(jnp.exp(heights), extent[axis_at] // parts).reshape((-1,) + (1,) * (len(extent) - 1 - axis_at))
    return factor_of


def normal_values(own_key, dims, scale, limit, cuts=(), held_as=jnp.bfloat16):
    entries = scale * jax.random.normal(own_key, dims, jnp.float32)
    if cuts:
        entries = entries * levels(own_key, dims, cuts, -0.22, 0.18)
    return jnp.clip(entries, -limit, limit).astype(held_as)


def setup_inputs(seed: int = 0) -> dict:
    seeds = jax.random.split(jax.random.key(seed), 10)
    return {
        "block_hidden_input": normal_values(seeds[0], (MICRO, TOKENS, MODEL_WIDTH), 1.0, 6.0, ((1, 32),)),
        "cached_score_gradient": normal_values(seeds[1], (MICRO, CANDS), 4.0, 24.0, ((1, 32),), jnp.float32),
        "value_projection": normal_values(seeds[2], (N_SECTION, MODEL_WIDTH, VALUE_WIDTH), MODEL_WIDTH ** -0.5, 0.0625, ((0, 8), (1, 32))),
        "output_projection": normal_values(seeds[3], (N_SECTION, VALUE_WIDTH, MODEL_WIDTH), VALUE_WIDTH ** -0.5, 0.25, ((0, 8), (2, 32))),
        "adapter_down_factor": normal_values(seeds[4], (N_SECTION, MODEL_WIDTH, ADAPTER_RANK), MODEL_WIDTH ** -0.5, 0.0625, ((0, 8), (1, 32))),
        "adapter_up_factor": normal_values(seeds[5], (N_SECTION, ADAPTER_RANK, VALUE_WIDTH), ADAPTER_RANK ** -0.5, 0.75, ((0, 8),)),
        "input_norm_gain": jnp.clip(1.0 + 0.1 * jax.random.normal(seeds[6], (N_SECTION, MODEL_WIDTH), jnp.float32), 0.5, 1.5),
        "last_norm_gain": jnp.clip(1.0 + 0.1 * jax.random.normal(seeds[7], (MODEL_WIDTH,), jnp.float32), 0.5, 1.5),
        "scoring_head_weight": normal_values(seeds[8], (MODEL_WIDTH,), MODEL_WIDTH ** -0.5, 0.0625, (), jnp.float32),
    }


ADAPTER_SCALE = 2.0
NORM_EPS = 1e-05

def normalize(hidden_state, input_norm_gain):
    values = hidden_state.astype(jnp.float32)
    factor = lax.rsqrt(lax.optimization_barrier(jnp.mean(values * values, axis=-1, keepdims=True)) + NORM_EPS)
    normalized_input = (values * factor * input_norm_gain).astype(jnp.bfloat16)
    return (values, factor, normalized_input)

def layer_forward_pass(hidden_state, input_norm_gain, value_projection, output_projection, adapter_down_factor, adapter_up_factor):
    values, factor, normalized_input = normalize(hidden_state, input_norm_gain)
    adapter_activation = jnp.dot(normalized_input, adapter_down_factor, preferred_element_type=jnp.float32).astype(jnp.bfloat16)
    value_projected = jnp.dot(normalized_input, value_projection, preferred_element_type=jnp.float32)
    value_projected = value_projected + ADAPTER_SCALE * jnp.dot(adapter_activation, adapter_up_factor, preferred_element_type=jnp.float32)
    value_projected = value_projected.astype(jnp.bfloat16)
    layer_result = (values + jnp.dot(value_projected, output_projection, preferred_element_type=jnp.float32)).astype(jnp.bfloat16)
    return (normalized_input, adapter_activation, layer_result)

def score_seed(hidden_state, last_norm_gain, scoring_head_weight, token_grads, length):
    values = hidden_state.astype(jnp.float32)
    factor = lax.rsqrt(lax.optimization_barrier(jnp.mean(values * values, axis=-1, keepdims=True)) + NORM_EPS)
    weighted = last_norm_gain * scoring_head_weight
    inner_sum = lax.optimization_barrier(jnp.sum(values * weighted, axis=-1, keepdims=True))
    columns = values.shape[-1]
    seed_grad = factor * weighted - factor * factor * factor * inner_sum * values / columns
    return (seed_grad * token_grads / length).astype(jnp.bfloat16)

def layer_backward_pass(hidden_state, following_gradient, input_norm_gain, value_projection, output_projection, adapter_down_factor, adapter_up_factor, normalized_input, adapter_activation):
    values, factor, unused = normalize(hidden_state, input_norm_gain)
    value_gradient = jnp.dot(following_gradient, output_projection.T, preferred_element_type=jnp.float32).astype(jnp.bfloat16)
    up_factor_term = ADAPTER_SCALE * jnp.dot(adapter_activation.T, value_gradient, preferred_element_type=jnp.float32)
    adapter_gradient = (ADAPTER_SCALE * jnp.dot(value_gradient, adapter_up_factor.T, preferred_element_type=jnp.float32)).astype(jnp.bfloat16)
    normalized_gradient = jnp.dot(value_gradient, value_projection.T, preferred_element_type=jnp.float32)
    normalized_gradient = normalized_gradient + jnp.dot(adapter_gradient, adapter_down_factor.T, preferred_element_type=jnp.float32)
    down_factor_term = jnp.dot(normalized_input.T, adapter_gradient, preferred_element_type=jnp.float32)
    scaled = normalized_gradient * input_norm_gain
    inner_sum = lax.optimization_barrier(jnp.sum(values * scaled, axis=-1, keepdims=True))
    columns = values.shape[-1]
    hidden_state_gradient = factor * scaled - factor * factor * factor * inner_sum * values / columns
    hidden_state_gradient = (following_gradient.astype(jnp.float32) + hidden_state_gradient).astype(jnp.bfloat16)
    return (hidden_state_gradient, down_factor_term, up_factor_term)

def reference(block_hidden_input, cached_score_gradient, value_projection, output_projection, adapter_down_factor, adapter_up_factor, input_norm_gain, last_norm_gain, scoring_head_weight):
    totals_down = [jnp.zeros((MODEL_WIDTH, ADAPTER_RANK), jnp.float32) for layer_number in range(N_SECTION)]
    totals_up = [jnp.zeros((ADAPTER_RANK, VALUE_WIDTH), jnp.float32) for layer_number in range(N_SECTION)]
    for block in range(MICRO):
        hidden_state = block_hidden_input[block]
        saved = []
        for layer_number in range(N_SECTION):
            normalized_input, adapter_activation, layer_result = layer_forward_pass(hidden_state, input_norm_gain[layer_number], value_projection[layer_number], output_projection[layer_number], adapter_down_factor[layer_number], adapter_up_factor[layer_number])
            saved.append((hidden_state, normalized_input, adapter_activation))
            hidden_state = layer_result
        token_grads = jnp.repeat(cached_score_gradient[block], TOK_DEV)[:, None]
        hidden_state_gradient = score_seed(hidden_state, last_norm_gain, scoring_head_weight, token_grads, TOK_DEV)
        for layer_number in range(N_SECTION - 1, -1, -1):
            layer_inputs, normalized_input, adapter_activation = saved[layer_number]
            hidden_state_gradient, down_factor_term, up_factor_term = layer_backward_pass(layer_inputs, hidden_state_gradient, input_norm_gain[layer_number], value_projection[layer_number], output_projection[layer_number], adapter_down_factor[layer_number], adapter_up_factor[layer_number], normalized_input, adapter_activation)
            totals_down[layer_number] = totals_down[layer_number] + down_factor_term
            totals_up[layer_number] = totals_up[layer_number] + up_factor_term
    return (jnp.stack(totals_down), jnp.stack(totals_up))
```

```python
import functools

import jax
import jax.numpy as jnp
from jax import lax
from jax.experimental import pallas as pl
from jax.experimental.pallas import tpu as pltpu
from jax.sharding import PartitionSpec as P

ADAPTER_SCALE = 2.0
NORM_EPS = 1e-05
NX = 4
MESH = pl.DeviceIdType.MESH
F32 = jnp.float32
BF16 = jnp.bfloat16


def dot_nn(a, b):
    return lax.dot_general(a, b, (((1,), (0,)), ((), ())), preferred_element_type=F32)


def dot_nt(a, b):
    return lax.dot_general(a, b, (((1,), (1,)), ((), ())), preferred_element_type=F32)


def dot_tn(a, b):
    return lax.dot_general(a, b, (((0,), (0,)), ((), ())), preferred_element_type=F32)


def two_parts(value):
    high = value.astype(BF16)
    low = (value - high.astype(F32)).astype(BF16)
    return high, low


def kernel(
    cfg,
    h_ref,
    o_ref,
    v_ref,
    a_ref,
    b_ref,
    g_ref,
    lg_ref,
    sw_ref,
    cg_ref,
    gd_ref,
    gu_ref,
    weights,
    states,
    grad,
    part,
    arrived,
    spread,
    totals,
    up_sums,
    scal,
    grad_out,
    grad_in,
    up_part,
    up_z,
    up_q,
    own_send,
    relay_send,
    core_send,
    weight_recv,
    h_send,
    h_recv,
    part_send,
    part_recv,
    spread_send,
    spread_recv,
    scal_send,
    scal_recv,
    grad_send,
    grad_recv,
    up_send,
    up_recv,
):
    NSEC, NZ, TOK, FB, VW, RANK, WIDTH, CANDLEN = cfg
    NY = NSEC // 2
    SLAB = 4 * FB
    ROWS = NZ * TOK
    UPR = RANK // 4
    QW = VW // FB
    R_V, R_A = VW, 2 * VW
    R_B = R_A + RANK
    R_G = R_B + UPR * QW
    R_END = R_G + 16
    SPLIT = (R_END // 32) * 16
    halves = (pl.ds(0, SPLIT), pl.ds(SPLIT, R_END - SPLIT))
    PW = VW + 128
    GROWS = RANK + UPR * QW

    sec = lax.axis_index("section")
    dp = lax.axis_index("dp")
    y, x_hi = sec // 2, sec % 2
    z, quarter = dp // 4, dp % 4
    x_lo, core = quarter // 2, quarter % 2
    x = x_hi * 2 + x_lo

    def device(xx, yy, zz, cc):
        return {"section": yy * 2 + xx // 2, "dp": zz * 4 + (xx % 2) * 2 + cc}

    def z_peer(d):
        zz = lax.rem(z + d, NZ)
        return zz, {"section": sec, "dp": zz * 4 + quarter}

    def place(xx, yy, cc):
        return yy * 2 + xx // 2, (xx % 2) * 2 + cc

    barrier = pltpu.get_barrier_semaphore()
    my_slot = sec * 4 + quarter

    def greet(slot, carry):
        @pl.when(slot != my_slot)
        def _():
            pl.semaphore_signal(
                barrier,
                inc=1,
                device_id={"section": slot // 4, "dp": z * 4 + slot % 4},
                device_id_type=MESH,
            )

        return carry

    lax.fori_loop(0, NSEC * 4, greet, 0)
    for d in range(1, NZ):
        pl.semaphore_signal(barrier, inc=1, device_id=z_peer(d)[1], device_id_type=MESH)
    pl.semaphore_wait(barrier, NSEC * 4 - 1 + NZ - 1)

    g_own = g_ref[:, pl.ds(pl.multiple_of(dp * FB, FB), FB)]
    g1, g1r = g_own.astype(BF16), g_own
    g_rest = g1r - g1.astype(F32)
    g2 = g_rest.astype(BF16)
    g3 = (g_rest - g2.astype(F32)).astype(BF16)
    row_id = lax.broadcasted_iota(jnp.int32, (16, FB), 0)
    g_rows = jnp.where(
        row_id == 0,
        g1.astype(F32),
        jnp.where(row_id == 1, g2.astype(F32), jnp.where(row_id == 2, g3.astype(F32), 0.0)),
    ).astype(BF16)
    weights[sec, quarter, 0:VW] = o_ref[...]
    weights[sec, quarter, R_V:R_A] = v_ref[...].T
    weights[sec, quarter, R_A:R_B] = a_ref[...].T
    up_rows = b_ref[pl.ds(pl.multiple_of(quarter * UPR, UPR), UPR), :]
    for w in range(QW):
        weights[sec, quarter, R_B + w * UPR : R_B + (w + 1) * UPR] = up_rows[
            :, w * FB : (w + 1) * FB
        ]
    weights[sec, quarter, R_G:R_END] = g_rows

    def weight_copy(xx, yy, half, target, send_sem):
        k, q = place(xx, yy, core)
        return pltpu.make_async_remote_copy(
            src_ref=weights.at[k, q, halves[half]],
            dst_ref=weights.at[k, q, halves[half]],
            send_sem=send_sem,
            recv_sem=weight_recv.at[k * 4 + q, half],
            device_id=target,
            device_id_type=MESH,
        )

    tok_row = pl.multiple_of(sec * TOK, TOK)

    def h_copy(d):
        zz, target = z_peer(d)
        return pltpu.make_async_remote_copy(
            src_ref=h_ref.at[pl.ds(tok_row, TOK), pl.ds(pl.multiple_of(zz * SLAB, SLAB), SLAB)],
            dst_ref=states.at[0, z],
            send_sem=h_send.at[d],
            recv_sem=h_recv.at[z],
            device_id=target,
            device_id_type=MESH,
        )

    sends = []
    own_states = pltpu.make_async_copy(
        h_ref.at[pl.ds(tok_row, TOK), pl.ds(pl.multiple_of(z * SLAB, SLAB), SLAB)],
        states.at[0, z],
        h_send.at[0],
    )
    own_states.start()
    for d in range(1, NZ):
        copy = h_copy(d)
        copy.start()
        sends.append(copy)

    for half in (0, 1):
        for i in range(1, NX):
            copy = weight_copy(
                x, y, half, device(lax.rem(x + i, NX), y, z, core), own_send.at[0, i, half]
            )
            copy.start()
            sends.append(copy)
        for j in range(1, NY):
            copy = weight_copy(
                x, y, 1 - half, device(x, lax.rem(y + j, NY), z, core), own_send.at[1, j, 1 - half]
            )
            copy.start()
            sends.append(copy)

    def weight_wait(k, q, rows, half):
        pltpu.make_async_copy(
            weights.at[k, q, rows], weights.at[k, q, rows], weight_recv.at[k * 4 + q, half]
        ).wait()

    for i in range(1, max(NX, NY)):
        if i < NX:
            xs = lax.rem(x + i, NX)
            k, q = place(xs, y, core)
            weight_wait(k, q, halves[0], 0)
            for j in range(1, NY):
                copy = weight_copy(
                    xs, y, 0, device(x, lax.rem(y + j, NY), z, core), relay_send.at[0, i, j]
                )
                copy.start()
                sends.append(copy)
        if i < NY:
            ys = lax.rem(y + i, NY)
            k, q = place(x, ys, core)
            weight_wait(k, q, halves[1], 1)
            for j in range(1, NX):
                copy = weight_copy(
                    x, ys, 1, device(lax.rem(x + j, NX), y, z, core), relay_send.at[1, i, j]
                )
                copy.start()
                sends.append(copy)

    whole = pl.ds(0, R_END)

    def core_copy(layer, lo):
        q = lo * 2 + core
        return pltpu.make_async_remote_copy(
            src_ref=weights.at[layer, q],
            dst_ref=weights.at[layer, q],
            send_sem=core_send.at[layer, lo],
            recv_sem=weight_recv.at[layer * 4 + q, 0],
            device_id=device(x, y, z, 1 - core),
            device_id_type=MESH,
        )

    def pass_on(layer):
        xs_hi, ys = layer % 2, layer // 2
        for lo in (0, 1):
            xs = xs_hi * 2 + lo
            q = lo * 2 + core

            @pl.when(ys != y)
            def _():
                weight_wait(layer, q, halves[0], 0)

            @pl.when(xs != x)
            def _():
                weight_wait(layer, q, halves[1], 1)

            core_copy(layer, lo).start()

    def take_over(layer):
        for lo in (0, 1):
            weight_wait(layer, lo * 2 + (1 - core), whole, 0)

    def gains(layer, q):
        return jnp.sum(weights[layer, q, R_G:R_END].astype(F32), axis=0, keepdims=True)

    def ups(layer):
        return [
            jnp.concatenate(
                [weights[layer, q, R_B + w * UPR : R_B + (w + 1) * UPR] for q in range(4)], axis=0
            )
            for w in range(QW)
        ]

    def part_copy(step, d):
        zz, target = z_peer(d)
        return pltpu.make_async_remote_copy(
            src_ref=part.at[zz],
            dst_ref=arrived.at[step, z],
            send_sem=part_send.at[d],
            recv_sem=part_recv.at[z],
            device_id=target,
            device_id_type=MESH,
        )

    def part_wait(step, d):
        zz = lax.rem(z + d, NZ)
        pltpu.make_async_copy(
            arrived.at[step, zz], arrived.at[step, zz], part_recv.at[zz]
        ).wait()

    def spread_copy(step, d):
        zz, target = z_peer(d)
        return pltpu.make_async_remote_copy(
            src_ref=spread.at[step, z],
            dst_ref=spread.at[step, z],
            send_sem=spread_send.at[d],
            recv_sem=spread_recv.at[z],
            device_id=target,
            device_id_type=MESH,
        )

    def spread_wait(step, d):
        zz = lax.rem(z + d, NZ)
        pltpu.make_async_copy(
            spread.at[step, zz], spread.at[step, zz], spread_recv.at[zz]
        ).wait()

    def exchange_start(step):
        for d in range(1, NZ):
            part_copy(step, d).start()

    def exchange_sum(step):
        for d in range(1, NZ):
            part_wait(step, d)
        total = part[z].astype(F32)
        for d in range(1, NZ):
            total = total + arrived[step, lax.rem(z + d, NZ)].astype(F32)
        return total

    def spread_all(step):
        for d in range(1, NZ):
            spread_copy(step, d).start()
        for d in range(1, NZ):
            part_copy(step, d).wait_send()
        for d in range(1, NZ):
            spread_wait(step, d)
        for d in range(1, NZ):
            spread_copy(step, d).wait_send()

    lane = lax.broadcasted_iota(jnp.int32, (ROWS, 128), 1)
    lane_own = lax.broadcasted_iota(jnp.int32, (TOK, 128), 1)

    def put_scalar(rank_part, scalar, lanes):
        high, low = two_parts(scalar)
        padded = jnp.concatenate([rank_part, jnp.zeros_like(rank_part)], axis=1)
        return jnp.where(
            lanes == RANK,
            high.astype(F32),
            jnp.where(lanes == RANK + 1, low.astype(F32), padded),
        )

    def get_scalar(tile, lanes):
        return jnp.sum(jnp.where(lanes >= RANK, tile, 0.0), axis=1, keepdims=True)

    pass_on(jnp.int32(0))
    own_states.wait()
    for d in range(1, NZ):
        zz = lax.rem(z + d, NZ)
        pltpu.make_async_copy(states.at[0, zz], states.at[0, zz], h_recv.at[zz]).wait()

    def forward_step(layer, carry):
        take_over(layer)
        ss = jnp.zeros((ROWS, 1), F32)
        value = jnp.zeros((ROWS, VW + RANK), F32)
        for q in range(4):
            xq = states[layer, :, :, q * FB : (q + 1) * FB].reshape(ROWS, FB).astype(F32)
            ss = ss + jnp.sum(xq * xq, axis=1, keepdims=True)
            xg = (xq * gains(layer, q)).astype(BF16)
            value = value + dot_nt(xg, weights[layer, q, R_V:R_B])
        part[:, :, 0:VW] = value[:, 0:VW].astype(BF16).reshape(NZ, TOK, VW)
        part[:, :, VW:PW] = (
            put_scalar(value[:, VW:], ss, lane).astype(BF16).reshape(NZ, TOK, 128)
        )
        exchange_start(layer)

        @pl.when(layer + 1 < NSEC)
        def _():
            pass_on(layer + 1)

        total = exchange_sum(layer)
        totals[layer] = total
        tail = total[:, VW:PW]
        r = lax.rsqrt(get_scalar(tail, lane_own) / WIDTH + NORM_EPS)
        t = (r * tail[:, 0:RANK]).astype(BF16)
        for w, up in enumerate(ups(layer)):
            cols = slice(w * FB, (w + 1) * FB)
            spread[layer, z, :, cols] = (
                r * total[:, cols] + ADAPTER_SCALE * dot_nn(t, up)
            ).astype(BF16)
        spread_all(layer)
        v = spread[layer, :, :, 0:VW].reshape(ROWS, VW)
        for q in range(4):
            cols = slice(q * FB, (q + 1) * FB)
            xq = states[layer, :, :, cols].reshape(ROWS, FB).astype(F32)
            states[layer + 1, :, :, cols] = (
                (xq + dot_nn(v, weights[layer, q, 0:VW])).astype(BF16).reshape(NZ, TOK, FB)
            )
        return carry

    lax.fori_loop(0, NSEC, forward_step, 0)

    slab = pl.ds(pl.multiple_of(z * SLAB, SLAB), SLAB)
    head = lg_ref[:, slab] * sw_ref[:, slab]
    last = states[NSEC].reshape(ROWS, SLAB).astype(F32)
    ss = jnp.sum(last * last, axis=1, keepdims=True)
    inner = jnp.sum(last * head, axis=1, keepdims=True)
    rows = lax.broadcasted_iota(jnp.int32, (ROWS, 128), 0)
    mine = jnp.logical_and(rows >= z * TOK, rows < (z + 1) * TOK)
    token_grad = jnp.where(mine, cg_ref[sec * TOK // CANDLEN, 0], 0.0)
    table = jnp.where(
        lane == 0, ss, jnp.where(lane == 1, inner, jnp.where(lane == 2, token_grad, 0.0))
    )
    scal[z] = table.T[0:8]

    def scal_copy(d):
        zz, target = z_peer(d)
        return pltpu.make_async_remote_copy(
            src_ref=scal.at[z],
            dst_ref=scal.at[z],
            send_sem=scal_send.at[d],
            recv_sem=scal_recv.at[z],
            device_id=target,
            device_id_type=MESH,
        )

    for d in range(1, NZ):
        copy = scal_copy(d)
        copy.start()
        sends.append(copy)
    for d in range(1, NZ):
        zz = lax.rem(z + d, NZ)
        pltpu.make_async_copy(scal.at[zz], scal.at[zz], scal_recv.at[zz]).wait()
    table = jnp.concatenate([jnp.sum(scal[...], axis=0)] * 16, axis=0).T
    if ROWS != 128:
        table = table[0:ROWS]
    ss = jnp.sum(jnp.where(lane == 0, table, 0.0), axis=1, keepdims=True)
    inner = jnp.sum(jnp.where(lane == 1, table, 0.0), axis=1, keepdims=True)
    token_grad = jnp.sum(jnp.where(lane == 2, table, 0.0), axis=1, keepdims=True)
    factor = lax.rsqrt(ss / WIDTH + NORM_EPS)
    token_grad = token_grad / CANDLEN
    grad[...] = (
        token_grad * factor * head
        - token_grad * factor * factor * factor * inner / WIDTH * last
    ).astype(BF16)

    def grad_copy(layer, q):
        return pltpu.make_async_remote_copy(
            src_ref=grad_out.at[layer, q],
            dst_ref=grad_in.at[my_slot],
            send_sem=grad_send.at[layer, q],
            recv_sem=grad_recv.at[my_slot],
            device_id={"section": layer, "dp": z * 4 + q},
            device_id_type=MESH,
        )

    def backward_step(index, carry):
        layer = NSEC - 1 - index
        step = NSEC + index
        value = jnp.zeros((ROWS, VW), F32)
        for q in range(4):
            value = value + dot_nt(grad[:, q * FB : (q + 1) * FB], weights[layer, q, 0:VW])
        part[:, :, 0:VW] = value.astype(BF16).reshape(NZ, TOK, VW)
        exchange_start(step)
        forward_total = totals[layer]
        tail = forward_total[:, VW:PW]
        r = lax.rsqrt(get_scalar(tail, lane_own) / WIDTH + NORM_EPS)
        t = (r * tail[:, 0:RANK]).astype(BF16)
        dv32 = exchange_sum(step)[:, 0:VW]
        dv = dv32.astype(BF16)
        dt32 = jnp.zeros((TOK, RANK), F32)
        for w, up in enumerate(ups(layer)):
            dt32 = dt32 + dot_nt(dv[:, w * FB : (w + 1) * FB], up)
        dt = (ADAPTER_SCALE * dt32).astype(BF16)
        dvf, dtf = dv.astype(F32), dt.astype(F32)
        inner = jnp.sum(dvf * forward_total[:, 0:VW], axis=1, keepdims=True) + jnp.sum(
            dtf * tail[:, 0:RANK], axis=1, keepdims=True
        )
        shrink = r * r * r * inner / WIDTH
        spread[step, z, :, 0:VW] = (r * dvf).astype(BF16)
        spread[step, z, :, VW:PW] = put_scalar(r * dtf, shrink, lane_own).astype(BF16)
        up_sums[...] = ADAPTER_SCALE * dot_tn(t, dv)
        spread_all(step)
        both = spread[step].reshape(ROWS, PW)
        scaled = both[:, 0 : VW + RANK]
        rdt = both[:, VW : VW + RANK]
        shrink = get_scalar(both[:, VW:PW].astype(F32), lane)
        for q in range(4):
            cols = slice(q * FB, (q + 1) * FB)
            xq = states[layer, :, :, cols].reshape(ROWS, FB)
            gq = gains(layer, q)
            grad_out[layer, q, 0:RANK] = (dot_tn(rdt, xq) * gq).astype(BF16)
            for w in range(QW):
                grad_out[layer, q, RANK + w * UPR : RANK + (w + 1) * UPR] = up_sums[
                    q * UPR : (q + 1) * UPR, w * FB : (w + 1) * FB
                ].astype(BF16)

            here = jnp.logical_and(layer == sec, quarter == q)

            @pl.when(jnp.logical_not(here))
            def _():
                grad_copy(layer, q).start()

            @pl.when(here)
            def _():
                grad_in[my_slot] = grad_out[layer, q]

        @pl.when(layer > 0)
        def _():
            for q in range(4):
                cols = slice(q * FB, (q + 1) * FB)
                xq = states[layer, :, :, cols].reshape(ROWS, FB).astype(F32)
                du = dot_nn(scaled, weights[layer, q, R_V:R_B])
                grad[:, cols] = (
                    grad[:, cols].astype(F32) + du * gains(layer, q) - shrink * xq
                ).astype(BF16)

        return carry

    lax.fori_loop(0, NSEC, backward_step, 0)

    def collect(slot, carry):
        @pl.when(slot != my_slot)
        def _():
            pltpu.make_async_copy(grad_in.at[slot], grad_in.at[slot], grad_recv.at[slot]).wait()

        return carry

    lax.fori_loop(0, NSEC * 4, collect, 0)
    summed = jnp.sum(grad_in[...].astype(F32), axis=0)
    up_z[z] = summed[RANK:GROWS].astype(BF16)
    for d in range(1, NZ):
        zz, target = z_peer(d)
        copy = pltpu.make_async_remote_copy(
            src_ref=up_z.at[z],
            dst_ref=up_z.at[z],
            send_sem=up_send.at[0, d],
            recv_sem=up_recv.at[0, z],
            device_id=target,
            device_id_type=MESH,
        )
        copy.start()
        sends.append(copy)
    gd_ref[...] = summed[0:RANK].T
    for d in range(1, NZ):
        zz = lax.rem(z + d, NZ)
        pltpu.make_async_copy(up_z.at[zz], up_z.at[zz], up_recv.at[0, zz]).wait()
    up_q[quarter] = jnp.sum(up_z[...].astype(F32), axis=0)
    for d in range(1, 4):
        copy = pltpu.make_async_remote_copy(
            src_ref=up_q.at[quarter],
            dst_ref=up_q.at[quarter],
            send_sem=up_send.at[1, d],
            recv_sem=up_recv.at[1, quarter],
            device_id={"section": sec, "dp": z * 4 + lax.rem(quarter + d, 4)},
            device_id_type=MESH,
        )
        copy.start()
        sends.append(copy)
    for d in range(1, 4):
        qq = lax.rem(quarter + d, 4)
        pltpu.make_async_copy(up_q.at[qq], up_q.at[qq], up_recv.at[1, qq]).wait()
    for q in range(4):
        for w in range(QW):
            gu_ref[q * UPR : (q + 1) * UPR, w * FB : (w + 1) * FB] = up_q[
                q, w * UPR : (w + 1) * UPR
            ]

    for copy in sends:
        copy.wait_send()

    def drain(layer, carry):
        for lo in (0, 1):
            core_copy(layer, lo).wait_send()
        for q in range(4):

            @pl.when(jnp.logical_not(jnp.logical_and(layer == sec, quarter == q)))
            def _():
                grad_copy(layer, q).wait_send()

        return carry

    lax.fori_loop(0, NSEC, drain, 0)


def per_device(
    block_hidden_input,
    cached_score_gradient,
    value_projection,
    output_projection,
    adapter_down_factor,
    adapter_up_factor,
    input_norm_gain,
    last_norm_gain,
    scoring_head_weight,
):
    nsec = lax.axis_size("section")
    nz = lax.axis_size("dp") // 4
    blocks, cand_len, width = block_hidden_input.shape
    tok = blocks * cand_len // nsec
    fb, vw = value_projection.shape[1:]
    rank = adapter_down_factor.shape[2]
    slab, rows = 4 * fb, nz * tok
    upr, qw = rank // 4, vw // fb
    r_end = 2 * vw + rank + upr * qw + 16
    pw = vw + 128
    grows = rank + upr * qw
    cfg = (nsec, nz, tok, fb, vw, rank, width, cand_len)
    vmem = pl.BlockSpec(memory_space=pltpu.VMEM)
    dma = pltpu.SemaphoreType.DMA
    grad_down, grad_up = pl.pallas_call(
        functools.partial(kernel, cfg),
        out_shape=(
            jax.ShapeDtypeStruct((fb, rank), F32),
            jax.ShapeDtypeStruct((rank, vw), F32),
        ),
        in_specs=[pl.BlockSpec(memory_space=pl.ANY)]
        + [vmem] * 7
        + [pl.BlockSpec(memory_space=pltpu.SMEM)],
        out_specs=(vmem, vmem),
        scratch_shapes=[
            pltpu.VMEM((nsec, 4, r_end, fb), BF16),
            pltpu.VMEM((nsec + 1, nz, tok, slab), BF16),
            pltpu.VMEM((rows, slab), BF16),
            pltpu.VMEM((nz, tok, pw), BF16),
            pltpu.VMEM((2 * nsec, nz, tok, pw), BF16),
            pltpu.VMEM((2 * nsec, nz, tok, pw), BF16),
            pltpu.VMEM((nsec, tok, pw), F32),
            pltpu.VMEM((rank, vw), F32),
            pltpu.VMEM((nz, 8, 128), F32),
            pltpu.VMEM((nsec, 4, grows, fb), BF16),
            pltpu.VMEM((nsec * 4, grows, fb), BF16),
            pltpu.VMEM((upr * qw, fb), F32),
            pltpu.VMEM((nz, upr * qw, fb), BF16),
            pltpu.VMEM((4, upr * qw, fb), F32),
            dma((2, 4, 2)),
            dma((2, 4, 4)),
            dma((nsec, 2)),
            dma((nsec * 4, 2)),
            dma((nz,)),
            dma((nz,)),
            dma((nz,)),
            dma((nz,)),
            dma((nz,)),
            dma((nz,)),
            dma((nz,)),
            dma((nz,)),
            dma((nsec, 4)),
            dma((nsec * 4,)),
            dma((2, 8)),
            dma((2, 8)),
        ],
        compiler_params=pltpu.CompilerParams(
            collective_id=0, has_side_effects=True, vmem_limit_bytes=56 * 1024 * 1024
        ),
        name="layers",
    )(
        block_hidden_input.reshape(blocks * cand_len, width),
        output_projection[0],
        value_projection[0],
        adapter_down_factor[0],
        adapter_up_factor[0],
        input_norm_gain,
        last_norm_gain.reshape(1, width),
        scoring_head_weight.reshape(1, width),
        cached_score_gradient,
    )
    return (grad_down[None], grad_up[None])


def solution(mesh):
    return jax.shard_map(
        per_device,
        mesh=mesh,
        in_specs=(
            P(None, "dp", None),
            P(None, "dp"),
            P("section", "dp", None),
            P("section", None, "dp"),
            P("section", "dp", None),
            P("section", None, None),
            P("section", None),
            P(),
            P(),
        ),
        out_specs=(P("section", "dp", None), P("section", None, None)),
        check_vma=False,
    )
```

```python
import functools

import jax
import jax.numpy as jnp
from jax import lax
from jax.experimental import pallas as pl
from jax.experimental.pallas import tpu as pltpu
from jax.sharding import PartitionSpec as P

ADAPTER_SCALE = 2.0
NORM_EPS = 1e-05
NX = 4
MESH = pl.DeviceIdType.MESH
F32 = jnp.float32
BF16 = jnp.bfloat16


def dot_nn(a, b):
    return lax.dot_general(a, b, (((1,), (0,)), ((), ())), preferred_element_type=F32)


def dot_nt(a, b):
    return lax.dot_general(a, b, (((1,), (1,)), ((), ())), preferred_element_type=F32)


def dot_tn(a, b):
    return lax.dot_general(a, b, (((0,), (0,)), ((), ())), preferred_element_type=F32)


def two_parts(value):
    high = value.astype(BF16)
    low = (value - high.astype(F32)).astype(BF16)
    return high, low


def kernel(
    cfg,
    h_ref,
    o_ref,
    v_ref,
    a_ref,
    b_ref,
    g_ref,
    lg_ref,
    sw_ref,
    cg_ref,
    gd_ref,
    gu_ref,
    weights,
    states,
    grad,
    part,
    arrived,
    spread,
    totals,
    down_sums,
    scal,
    grad_out,
    grad_in,
    up_z,
    up_q,
    own_send,
    relay_send,
    core_send,
    weight_recv,
    h_send,
    h_recv,
    part_send,
    part_recv,
    spread_send,
    spread_recv,
    scal_send,
    scal_recv,
    grad_send,
    grad_recv,
    up_send,
    up_recv,
):
    NSEC, NZ, TOK, FB, VW, RANK, WIDTH, CANDLEN = cfg
    NY = NSEC // 2
    SLAB = 4 * FB
    ROWS = NZ * TOK
    UPR = RANK // 4
    QW = VW // FB
    R_V, R_A = VW, 2 * VW
    R_B = R_A + RANK
    R_G = R_B + UPR * QW
    R_END = R_G + 16
    SPLIT = (R_END // 32) * 16
    halves = (pl.ds(0, SPLIT), pl.ds(SPLIT, R_END - SPLIT))
    PW = VW + 128
    GROWS = RANK + UPR * QW

    sec = lax.axis_index("section")
    dp = lax.axis_index("dp")
    y, x_hi = sec // 2, sec % 2
    z, quarter = dp // 4, dp % 4
    x_lo, core = quarter // 2, quarter % 2
    x = x_hi * 2 + x_lo

    def device(xx, yy, zz, cc):
        return {"section": yy * 2 + xx // 2, "dp": zz * 4 + (xx % 2) * 2 + cc}

    def z_peer(d):
        zz = lax.rem(z + d, NZ)
        return zz, {"section": sec, "dp": zz * 4 + quarter}

    def place(xx, yy, cc):
        return yy * 2 + xx // 2, (xx % 2) * 2 + cc

    barrier = pltpu.get_barrier_semaphore()
    my_slot = sec * 4 + quarter

    def greet(slot, carry):
        @pl.when(slot != my_slot)
        def _():
            pl.semaphore_signal(
                barrier,
                inc=1,
                device_id={"section": slot // 4, "dp": z * 4 + slot % 4},
                device_id_type=MESH,
            )

        return carry

    lax.fori_loop(0, NSEC * 4, greet, 0)
    for d in range(1, NZ):
        pl.semaphore_signal(barrier, inc=1, device_id=z_peer(d)[1], device_id_type=MESH)
    pl.semaphore_wait(barrier, NSEC * 4 - 1 + NZ - 1)

    g_own = g_ref[:, pl.ds(pl.multiple_of(dp * FB, FB), FB)]
    g1, g1r = g_own.astype(BF16), g_own
    g_rest = g1r - g1.astype(F32)
    g2 = g_rest.astype(BF16)
    g3 = (g_rest - g2.astype(F32)).astype(BF16)
    row_id = lax.broadcasted_iota(jnp.int32, (16, FB), 0)
    g_rows = jnp.where(
        row_id == 0,
        g1.astype(F32),
        jnp.where(row_id == 1, g2.astype(F32), jnp.where(row_id == 2, g3.astype(F32), 0.0)),
    ).astype(BF16)
    weights[sec, quarter, 0:VW] = o_ref[...]
    weights[sec, quarter, R_V:R_A] = v_ref[...].T
    weights[sec, quarter, R_A:R_B] = a_ref[...].T
    up_rows = b_ref[pl.ds(pl.multiple_of(quarter * UPR, UPR), UPR), :]
    for w in range(QW):
        weights[sec, quarter, R_B + w * UPR : R_B + (w + 1) * UPR] = up_rows[
            :, w * FB : (w + 1) * FB
        ]
    weights[sec, quarter, R_G:R_END] = g_rows

    def weight_copy(xx, yy, half, target, send_sem):
        k, q = place(xx, yy, core)
        return pltpu.make_async_remote_copy(
            src_ref=weights.at[k, q, halves[half]],
            dst_ref=weights.at[k, q, halves[half]],
            send_sem=send_sem,
            recv_sem=weight_recv.at[k * 4 + q, half],
            device_id=target,
            device_id_type=MESH,
        )

    tok_row = pl.multiple_of(sec * TOK, TOK)
    HALF = NZ // 2
    SR = HALF * TOK
    stream, owner = z % 2, z // 2
    my_rows = stream * HALF + owner

    def slot_of(zz):
        return (zz % 2) * HALF + zz // 2

    sends = []
    own_states = pltpu.make_async_copy(
        h_ref.at[pl.ds(tok_row, TOK), pl.ds(pl.multiple_of(z * SLAB, SLAB), SLAB)],
        states.at[0, my_rows],
        h_send.at[0],
    )
    own_states.start()
    for d in range(1, NZ):
        zz, target = z_peer(d)
        copy = pltpu.make_async_remote_copy(
            src_ref=h_ref.at[pl.ds(tok_row, TOK), pl.ds(pl.multiple_of(zz * SLAB, SLAB), SLAB)],
            dst_ref=states.at[0, my_rows],
            send_sem=h_send.at[d],
            recv_sem=h_recv.at[z],
            device_id=target,
            device_id_type=MESH,
        )
        copy.start()
        sends.append(copy)

    def weight_wait(k, q, rows, half):
        pltpu.make_async_copy(
            weights.at[k, q, rows], weights.at[k, q, rows], weight_recv.at[k * 4 + q, half]
        ).wait()

    def after(i, n):
        return lax.rem(i + 1, n)

    def before(i, n):
        return lax.rem(i + n - 1, n)

    y_next, y_prev, x_next, x_prev = after(y, NY), before(y, NY), after(x, NX), before(x, NX)

    def column_copies():
        up, down = device(x, y_next, z, core), device(x, y_prev, z, core)
        return [
            weight_copy(x, y, half, target, own_send.at[i])
            for i, (half, target) in enumerate(((0, up), (1, down), (1, up), (0, down)))
        ]

    def column_relays():
        return [
            weight_copy(x, y_prev, 0, device(x, y_next, z, core), own_send.at[4]),
            weight_copy(x, y_next, 1, device(x, y_prev, z, core), own_send.at[5]),
        ]

    def row_copies(ys):
        right, left = device(x_next, y, z, core), device(x_prev, y, z, core)
        return [
            weight_copy(x, ys, half, target, relay_send.at[ys, i])
            for i, (half, target) in enumerate(((0, right), (1, left), (1, right), (0, left)))
        ]

    def row_relays(ys):
        return [
            weight_copy(x_prev, ys, 0, device(x_next, y, z, core), relay_send.at[ys, 4]),
            weight_copy(x_next, ys, 1, device(x_prev, y, z, core), relay_send.at[ys, 5]),
        ]

    def row_send(ys):
        k, q = place(x, ys, core)

        @pl.when(jnp.logical_and(ys != y, ys != y_prev))
        def _():
            weight_wait(k, q, halves[0], 0)

        @pl.when(jnp.logical_and(ys != y, ys != y_next))
        def _():
            weight_wait(k, q, halves[1], 1)

        for copy in row_copies(ys):
            copy.start()

    def row_relay(ys):
        first, second = row_relays(ys)
        k, q = place(x_prev, ys, core)
        weight_wait(k, q, halves[0], 0)
        first.start()
        k, q = place(x_next, ys, core)
        weight_wait(k, q, halves[1], 1)
        second.start()

    if NY > 1:
        for copy in column_copies():
            copy.start()
        first, second = column_relays()
        k, q = place(x, y_prev, core)
        weight_wait(k, q, halves[0], 0)
        first.start()
        k, q = place(x, y_next, core)
        weight_wait(k, q, halves[1], 1)
        second.start()
    for ys in range(NY):
        row_send(ys)
    row_relay(0)

    whole = pl.ds(0, R_END)

    def core_copy(layer, lo):
        q = lo * 2 + core
        return pltpu.make_async_remote_copy(
            src_ref=weights.at[layer, q],
            dst_ref=weights.at[layer, q],
            send_sem=core_send.at[layer, lo],
            recv_sem=weight_recv.at[layer * 4 + q, 0],
            device_id=device(x, y, z, 1 - core),
            device_id_type=MESH,
        )

    def pass_on(layer):
        for lo in (0, 1):
            xs = (layer % 2) * 2 + lo
            q = lo * 2 + core

            @pl.when(jnp.logical_and(xs != x, xs != x_prev))
            def _():
                weight_wait(layer, q, halves[0], 0)

            @pl.when(jnp.logical_and(xs != x, xs != x_next))
            def _():
                weight_wait(layer, q, halves[1], 1)

            core_copy(layer, lo).start()

    def take_over(layer):
        for lo in (0, 1):
            weight_wait(layer, lo * 2 + (1 - core), whole, 0)

    def gains(layer, q):
        return jnp.sum(weights[layer, q, R_G:R_END].astype(F32), axis=0, keepdims=True)

    def ups(layer):
        return [
            jnp.concatenate(
                [weights[layer, q, R_B + w * UPR : R_B + (w + 1) * UPR] for q in range(4)], axis=0
            )
            for w in range(QW)
        ]

    def peer(st, d):
        zz = 2 * lax.rem(owner + d, HALF) + st
        return zz, {"section": sec, "dp": zz * 4 + quarter}

    def part_copy(st, step, d, lanes):
        zz, target = peer(st, d)
        return pltpu.make_async_remote_copy(
            src_ref=part.at[st, zz // 2, :, pl.ds(0, lanes)],
            dst_ref=arrived.at[step, z, :, pl.ds(0, lanes)],
            send_sem=part_send.at[st, d],
            recv_sem=part_recv.at[z],
            device_id=target,
            device_id_type=MESH,
        )

    def spread_copy(step, d, lanes):
        target = z_peer(d)[1]
        return pltpu.make_async_remote_copy(
            src_ref=spread.at[step, my_rows, :, pl.ds(0, lanes)],
            dst_ref=spread.at[step, my_rows, :, pl.ds(0, lanes)],
            send_sem=spread_send.at[d],
            recv_sem=spread_recv.at[z],
            device_id=target,
            device_id_type=MESH,
        )

    def exchange_start(st, step, lanes):
        @pl.when(stream != st)
        def _():
            part_copy(st, step, 0, lanes).start()

        for d in range(1, HALF):
            part_copy(st, step, d, lanes).start()

    def exchange_sum(st, step, lanes):
        for d in range(1, NZ):
            zz = lax.rem(z + d, NZ)
            ref = arrived.at[step, zz, :, pl.ds(0, lanes)]
            pltpu.make_async_copy(ref, ref, part_recv.at[zz]).wait()
        total = part[st, owner, :, 0:lanes].astype(F32)
        for d in range(1, NZ):
            total = total + arrived[step, lax.rem(z + d, NZ), :, 0:lanes].astype(F32)
        return total

    def spread_start(step, lanes):
        for d in range(1, NZ):
            spread_copy(step, d, lanes).start()

    def exchange_end(st, step, part_lanes, lanes):
        @pl.when(stream != st)
        def _():
            part_copy(st, step, 0, part_lanes).wait_send()

        for d in range(1, HALF):
            part_copy(st, step, d, part_lanes).wait_send()

        def arrive(d):
            zz = peer(st, d)[0]
            ref = spread.at[step, slot_of(zz), :, pl.ds(0, lanes)]
            pltpu.make_async_copy(ref, ref, spread_recv.at[zz]).wait()

        @pl.when(stream != st)
        def _():
            arrive(0)

        for d in range(1, HALF):
            arrive(d)

        @pl.when(stream == st)
        def _():
            for d in range(1, NZ):
                spread_copy(step, d, lanes).wait_send()

    lane_stream = lax.broadcasted_iota(jnp.int32, (SR, 128), 1)
    lane = lax.broadcasted_iota(jnp.int32, (ROWS, 128), 1)
    lane_own = lax.broadcasted_iota(jnp.int32, (TOK, 128), 1)

    def put_scalar(rank_part, scalar, lanes):
        high, low = two_parts(scalar)
        padded = jnp.concatenate([rank_part, jnp.zeros_like(rank_part)], axis=1)
        return jnp.where(
            lanes == RANK,
            high.astype(F32),
            jnp.where(lanes == RANK + 1, low.astype(F32), padded),
        )

    def get_scalar(tile, lanes):
        return jnp.sum(jnp.where(lanes >= RANK, tile, 0.0), axis=1, keepdims=True)

    pass_on(jnp.int32(0))
    own_states.wait()
    for d in range(1, NZ):
        zz = lax.rem(z + d, NZ)
        ref = states.at[0, slot_of(zz)]
        pltpu.make_async_copy(ref, ref, h_recv.at[zz]).wait()

    def rows_of(layer, st, q):
        own_rows = slice(st * HALF, (st + 1) * HALF)
        return states[layer, own_rows, :, q * FB : (q + 1) * FB].reshape(SR, FB)

    def forward_part(st, layer):
        ss = jnp.zeros((SR, 1), F32)
        value = jnp.zeros((SR, VW + RANK), F32)
        for q in range(4):
            xq = rows_of(layer, st, q).astype(F32)
            ss = ss + jnp.sum(xq * xq, axis=1, keepdims=True)
            xg = (xq * gains(layer, q)).astype(BF16)
            value = value + dot_nt(xg, weights[layer, q, R_V:R_B])
        part[st, :, :, 0:VW] = value[:, 0:VW].astype(BF16).reshape(HALF, TOK, VW)
        part[st, :, :, VW:PW] = (
            put_scalar(value[:, VW:], ss, lane_stream).astype(BF16).reshape(HALF, TOK, 128)
        )
        exchange_start(st, layer, PW)

    def forward_own(st, layer):
        @pl.when(stream == st)
        def _():
            total = exchange_sum(st, layer, PW)
            totals[layer] = total
            tail = total[:, VW:PW]
            r = lax.rsqrt(get_scalar(tail, lane_own) / WIDTH + NORM_EPS)
            t = (r * tail[:, 0:RANK]).astype(BF16)
            for w, up in enumerate(ups(layer)):
                cols = slice(w * FB, (w + 1) * FB)
                spread[layer, my_rows, :, cols] = (
                    r * total[:, cols] + ADAPTER_SCALE * dot_nn(t, up)
                ).astype(BF16)
            spread_start(layer, VW)

    def forward_end(st, layer):
        exchange_end(st, layer, PW, VW)
        own_rows = slice(st * HALF, (st + 1) * HALF)
        v = spread[layer, own_rows, :, 0:VW].reshape(SR, VW)
        for q in range(4):
            xq = rows_of(layer, st, q).astype(F32)
            states[layer + 1, own_rows, :, q * FB : (q + 1) * FB] = (
                (xq + dot_nn(v, weights[layer, q, 0:VW])).astype(BF16).reshape(HALF, TOK, FB)
            )

    take_over(jnp.int32(0))
    forward_part(0, jnp.int32(0))

    def forward_step(layer, carry):
        @pl.when(layer > 0)
        def _():
            forward_end(1, layer - 1)

        forward_part(1, layer)

        @pl.when(jnp.logical_and(layer % 2 == 0, layer // 2 + 1 < NY))
        def _():
            row_relay(layer // 2 + 1)

        forward_own(0, layer)
        forward_own(1, layer)

        @pl.when(layer + 1 < NSEC)
        def _():
            pass_on(layer + 1)

        forward_end(0, layer)

        @pl.when(layer + 1 < NSEC)
        def _():
            take_over(layer + 1)
            forward_part(0, layer + 1)

        return carry

    lax.fori_loop(0, NSEC, forward_step, 0)
    forward_end(1, jnp.int32(NSEC - 1))

    slab = pl.ds(pl.multiple_of(z * SLAB, SLAB), SLAB)
    head = lg_ref[:, slab] * sw_ref[:, slab]
    last = states[NSEC].reshape(ROWS, SLAB).astype(F32)
    ss = jnp.sum(last * last, axis=1, keepdims=True)
    inner = jnp.sum(last * head, axis=1, keepdims=True)
    rows = lax.broadcasted_iota(jnp.int32, (ROWS, 128), 0)
    mine = jnp.logical_and(rows >= my_rows * TOK, rows < (my_rows + 1) * TOK)
    token_grad = jnp.where(mine, cg_ref[sec * TOK // CANDLEN, 0], 0.0)
    table = jnp.where(
        lane == 0, ss, jnp.where(lane == 1, inner, jnp.where(lane == 2, token_grad, 0.0))
    )
    if ROWS != 128:
        table = jnp.concatenate([table] * (128 // ROWS), axis=0)
    scal[z] = table.T[0:8]

    def scal_copy(d):
        zz, target = z_peer(d)
        return pltpu.make_async_remote_copy(
            src_ref=scal.at[z],
            dst_ref=scal.at[z],
            send_sem=scal_send.at[d],
            recv_sem=scal_recv.at[z],
            device_id=target,
            device_id_type=MESH,
        )

    for d in range(1, NZ):
        copy = scal_copy(d)
        copy.start()
        sends.append(copy)
    for d in range(1, NZ):
        zz = lax.rem(z + d, NZ)
        pltpu.make_async_copy(scal.at[zz], scal.at[zz], scal_recv.at[zz]).wait()
    table = jnp.concatenate([jnp.sum(scal[...], axis=0)] * 16, axis=0).T
    if ROWS != 128:
        table = table[0:ROWS]
    ss = jnp.sum(jnp.where(lane == 0, table, 0.0), axis=1, keepdims=True)
    inner = jnp.sum(jnp.where(lane == 1, table, 0.0), axis=1, keepdims=True)
    token_grad = jnp.sum(jnp.where(lane == 2, table, 0.0), axis=1, keepdims=True)
    factor = lax.rsqrt(ss / WIDTH + NORM_EPS)
    token_grad = token_grad / CANDLEN
    grad[...] = (
        token_grad * factor * head
        - token_grad * factor * factor * factor * inner / WIDTH * last
    ).astype(BF16)

    def grad_copy(layer, q):
        return pltpu.make_async_remote_copy(
            src_ref=grad_out.at[layer, q],
            dst_ref=grad_in.at[my_slot],
            send_sem=grad_send.at[layer, q],
            recv_sem=grad_recv.at[my_slot],
            device_id={"section": layer, "dp": z * 4 + q},
            device_id_type=MESH,
        )

    def backward_part(st, layer):
        value = jnp.zeros((SR, VW), F32)
        for q in range(4):
            value = value + dot_nt(
                grad[st * SR : (st + 1) * SR, q * FB : (q + 1) * FB], weights[layer, q, 0:VW]
            )
        part[st, :, :, 0:VW] = value.astype(BF16).reshape(HALF, TOK, VW)
        exchange_start(st, 2 * NSEC - 1 - layer, VW)

    def backward_own(st, layer):
        step = 2 * NSEC - 1 - layer

        @pl.when(stream == st)
        def _():
            forward_total = totals[layer]
            tail = forward_total[:, VW:PW]
            r = lax.rsqrt(get_scalar(tail, lane_own) / WIDTH + NORM_EPS)
            t = (r * tail[:, 0:RANK]).astype(BF16)
            dv = exchange_sum(st, step, VW).astype(BF16)
            dt32 = jnp.zeros((TOK, RANK), F32)
            for w, up in enumerate(ups(layer)):
                dt32 = dt32 + dot_nt(dv[:, w * FB : (w + 1) * FB], up)
            dt = (ADAPTER_SCALE * dt32).astype(BF16)
            dvf, dtf = dv.astype(F32), dt.astype(F32)
            inner = jnp.sum(dvf * forward_total[:, 0:VW], axis=1, keepdims=True) + jnp.sum(
                dtf * tail[:, 0:RANK], axis=1, keepdims=True
            )
            shrink = r * r * r * inner / WIDTH
            spread[step, my_rows, :, 0:VW] = (r * dvf).astype(BF16)
            spread[step, my_rows, :, VW:PW] = put_scalar(r * dtf, shrink, lane_own).astype(BF16)
            spread_start(step, PW)
            up_sum = (ADAPTER_SCALE * dot_tn(t, dv)).astype(BF16)
            for q in range(4):
                for w in range(QW):
                    grad_out[layer, q, RANK + w * UPR : RANK + (w + 1) * UPR] = up_sum[
                        q * UPR : (q + 1) * UPR, w * FB : (w + 1) * FB
                    ]

    def backward_end(st, layer):
        step = 2 * NSEC - 1 - layer
        exchange_end(st, step, VW, PW)
        both = spread[step, st * HALF : (st + 1) * HALF].reshape(SR, PW)
        scaled = both[:, 0 : VW + RANK]
        shrink = get_scalar(both[:, VW:PW].astype(F32), lane_stream)
        own_rows = slice(st * SR, (st + 1) * SR)

        @pl.when(layer > 0)
        def _():
            for q in range(4):
                cols = slice(q * FB, (q + 1) * FB)
                du = dot_nn(scaled, weights[layer, q, R_V:R_B])
                grad[own_rows, cols] = (
                    grad[own_rows, cols].astype(F32)
                    + du * gains(layer, q)
                    - shrink * rows_of(layer, st, q).astype(F32)
                ).astype(BF16)

    def backward_sums(st, layer):
        step = 2 * NSEC - 1 - layer
        rdt = spread[step, st * HALF : (st + 1) * HALF, :, VW : VW + RANK].reshape(SR, RANK)
        for q in range(4):
            share = dot_tn(rdt, rows_of(layer, st, q)) * gains(layer, q)
            if st == 0:
                down_sums[q] = share
                continue
            grad_out[layer, q, 0:RANK] = (down_sums[q] + share).astype(BF16)
            here = jnp.logical_and(layer == sec, quarter == q)

            @pl.when(jnp.logical_not(here))
            def _():
                grad_copy(layer, q).start()

            @pl.when(here)
            def _():
                grad_in[my_slot] = grad_out[layer, q]

    backward_part(0, jnp.int32(NSEC - 1))

    def backward_step(index, carry):
        layer = NSEC - 1 - index

        @pl.when(index > 0)
        def _():
            backward_end(1, layer + 1)

        backward_part(1, layer)

        @pl.when(index > 0)
        def _():
            backward_sums(1, layer + 1)

        backward_own(0, layer)
        backward_own(1, layer)
        backward_end(0, layer)

        @pl.when(layer > 0)
        def _():
            backward_part(0, layer - 1)

        backward_sums(0, layer)
        return carry

    lax.fori_loop(0, NSEC, backward_step, 0)
    backward_end(1, jnp.int32(0))
    backward_sums(1, jnp.int32(0))

    def collect(slot, carry):
        @pl.when(slot != my_slot)
        def _():
            pltpu.make_async_copy(grad_in.at[slot], grad_in.at[slot], grad_recv.at[slot]).wait()

        return carry

    lax.fori_loop(0, NSEC * 4, collect, 0)
    summed = jnp.sum(grad_in[...].astype(F32), axis=0)
    up_z[z] = summed[RANK:GROWS].astype(BF16)
    for d in range(1, NZ):
        zz, target = z_peer(d)
        copy = pltpu.make_async_remote_copy(
            src_ref=up_z.at[z],
            dst_ref=up_z.at[z],
            send_sem=up_send.at[0, d],
            recv_sem=up_recv.at[0, z],
            device_id=target,
            device_id_type=MESH,
        )
        copy.start()
        sends.append(copy)
    gd_ref[...] = summed[0:RANK].T
    for d in range(1, NZ):
        zz = lax.rem(z + d, NZ)
        pltpu.make_async_copy(up_z.at[zz], up_z.at[zz], up_recv.at[0, zz]).wait()
    up_q[quarter] = jnp.sum(up_z[...].astype(F32), axis=0)
    for d in range(1, 4):
        copy = pltpu.make_async_remote_copy(
            src_ref=up_q.at[quarter],
            dst_ref=up_q.at[quarter],
            send_sem=up_send.at[1, d],
            recv_sem=up_recv.at[1, quarter],
            device_id={"section": sec, "dp": z * 4 + lax.rem(quarter + d, 4)},
            device_id_type=MESH,
        )
        copy.start()
        sends.append(copy)
    for d in range(1, 4):
        qq = lax.rem(quarter + d, 4)
        pltpu.make_async_copy(up_q.at[qq], up_q.at[qq], up_recv.at[1, qq]).wait()
    for q in range(4):
        for w in range(QW):
            gu_ref[q * UPR : (q + 1) * UPR, w * FB : (w + 1) * FB] = up_q[
                q, w * UPR : (w + 1) * UPR
            ]

    for copy in sends:
        copy.wait_send()
    if NY > 1:
        for copy in column_copies() + column_relays():
            copy.wait_send()
    for ys in range(NY):
        for copy in row_copies(ys) + row_relays(ys):
            copy.wait_send()

    def drain(layer, carry):
        for lo in (0, 1):
            core_copy(layer, lo).wait_send()
        for q in range(4):

            @pl.when(jnp.logical_not(jnp.logical_and(layer == sec, quarter == q)))
            def _():
                grad_copy(layer, q).wait_send()

        return carry

    lax.fori_loop(0, NSEC, drain, 0)


def per_device(
    block_hidden_input,
    cached_score_gradient,
    value_projection,
    output_projection,
    adapter_down_factor,
    adapter_up_factor,
    input_norm_gain,
    last_norm_gain,
    scoring_head_weight,
):
    nsec = lax.axis_size("section")
    nz = lax.axis_size("dp") // 4
    blocks, cand_len, width = block_hidden_input.shape
    tok = blocks * cand_len // nsec
    fb, vw = value_projection.shape[1:]
    rank = adapter_down_factor.shape[2]
    slab, rows = 4 * fb, nz * tok
    upr, qw = rank // 4, vw // fb
    r_end = 2 * vw + rank + upr * qw + 16
    pw = vw + 128
    grows = rank + upr * qw
    cfg = (nsec, nz, tok, fb, vw, rank, width, cand_len)
    vmem = pl.BlockSpec(memory_space=pltpu.VMEM)
    dma = pltpu.SemaphoreType.DMA
    grad_down, grad_up = pl.pallas_call(
        functools.partial(kernel, cfg),
        out_shape=(
            jax.ShapeDtypeStruct((fb, rank), F32),
            jax.ShapeDtypeStruct((rank, vw), F32),
        ),
        in_specs=[pl.BlockSpec(memory_space=pl.ANY)]
        + [vmem] * 7
        + [pl.BlockSpec(memory_space=pltpu.SMEM)],
        out_specs=(vmem, vmem),
        scratch_shapes=[
            pltpu.VMEM((nsec, 4, r_end, fb), BF16),
            pltpu.VMEM((nsec + 1, nz, tok, slab), BF16),
            pltpu.VMEM((rows, slab), BF16),
            pltpu.VMEM((2, nz // 2, tok, pw), BF16),
            pltpu.VMEM((2 * nsec, nz, tok, pw), BF16),
            pltpu.VMEM((2 * nsec, nz, tok, pw), BF16),
            pltpu.VMEM((nsec, tok, pw), F32),
            pltpu.VMEM((4, rank, fb), F32),
            pltpu.VMEM((nz, 8, 128), F32),
            pltpu.VMEM((nsec, 4, grows, fb), BF16),
            pltpu.VMEM((nsec * 4, grows, fb), BF16),
            pltpu.VMEM((nz, upr * qw, fb), BF16),
            pltpu.VMEM((4, upr * qw, fb), F32),
            dma((6,)),
            dma((nsec // 2, 6)),
            dma((nsec, 2)),
            dma((nsec * 4, 2)),
            dma((nz,)),
            dma((nz,)),
            dma((2, nz)),
            dma((nz,)),
            dma((nz,)),
            dma((nz,)),
            dma((nz,)),
            dma((nz,)),
            dma((nsec, 4)),
            dma((nsec * 4,)),
            dma((2, 8)),
            dma((2, 8)),
        ],
        compiler_params=pltpu.CompilerParams(
            collective_id=0, has_side_effects=True, vmem_limit_bytes=56 * 1024 * 1024
        ),
        name="layers",
    )(
        block_hidden_input.reshape(blocks * cand_len, width),
        output_projection[0],
        value_projection[0],
        adapter_down_factor[0],
        adapter_up_factor[0],
        input_norm_gain,
        last_norm_gain.reshape(1, width),
        scoring_head_weight.reshape(1, width),
        cached_score_gradient,
    )
    return (grad_down[None], grad_up[None])


def solution(mesh):
    return jax.shard_map(
        per_device,
        mesh=mesh,
        in_specs=(
            P(None, "dp", None),
            P(None, "dp"),
            P("section", "dp", None),
            P("section", None, "dp"),
            P("section", "dp", None),
            P("section", None, None),
            P("section", None),
            P(),
            P(),
        ),
        out_specs=(P("section", "dp", None), P("section", None, None)),
        check_vma=False,
    )
```

```python
import functools

import jax
import jax.numpy as jnp
from jax import lax
from jax.experimental import pallas as pl
from jax.experimental.pallas import tpu as pltpu
from jax.sharding import PartitionSpec as P

ADAPTER_SCALE = 2.0
NORM_EPS = 1e-05
NX = 4
MESH = pl.DeviceIdType.MESH
F32 = jnp.float32
BF16 = jnp.bfloat16


def dot_nn(a, b):
    return lax.dot_general(a, b, (((1,), (0,)), ((), ())), preferred_element_type=F32)


def dot_nt(a, b):
    return lax.dot_general(a, b, (((1,), (1,)), ((), ())), preferred_element_type=F32)


def dot_tn(a, b):
    return lax.dot_general(a, b, (((0,), (0,)), ((), ())), preferred_element_type=F32)


def two_parts(value):
    high = value.astype(BF16)
    low = (value - high.astype(F32)).astype(BF16)
    return high, low


def kernel(
    cfg,
    h_ref,
    o_ref,
    v_ref,
    a_ref,
    b_ref,
    g_ref,
    lg_ref,
    sw_ref,
    cg_ref,
    gd_ref,
    gu_ref,
    weights,
    states,
    grad,
    part,
    arrived,
    spread,
    totals,
    down_sums,
    scal,
    grad_out,
    grad_in,
    up_z,
    up_q,
    own_send,
    relay_send,
    core_send,
    weight_recv,
    h_send,
    h_recv,
    part_send,
    part_recv,
    spread_send,
    spread_recv,
    scal_send,
    scal_recv,
    grad_send,
    grad_recv,
    up_send,
    up_recv,
):
    NSEC, NZ, TOK, FB, VW, RANK, WIDTH, CANDLEN = cfg
    NY = NSEC // 2
    SLAB = 4 * FB
    ROWS = NZ * TOK
    UPR = RANK // 4
    QW = VW // FB
    R_V, R_A = VW, 2 * VW
    R_B = R_A + RANK
    R_G = R_B + UPR * QW
    R_END = -(-(R_G + 16) // 32) * 32
    SPLIT = R_END // 2
    PW = VW + 128
    GROWS = RANK + UPR * QW

    sec = lax.axis_index("section")
    dp = lax.axis_index("dp")
    y, x_hi = sec // 2, sec % 2
    z, quarter = dp // 4, dp % 4
    x_lo, core = quarter // 2, quarter % 2
    x = x_hi * 2 + x_lo

    def device(xx, yy, zz, cc):
        return {"section": yy * 2 + xx // 2, "dp": zz * 4 + (xx % 2) * 2 + cc}

    def z_peer(d):
        zz = lax.rem(z + d, NZ)
        return zz, {"section": sec, "dp": zz * 4 + quarter}

    def place(xx, yy, cc):
        return yy * 2 + xx // 2, (xx % 2) * 2 + cc

    barrier = pltpu.get_barrier_semaphore()
    my_slot = sec * 4 + quarter

    def greet(slot, carry):
        @pl.when(slot != my_slot)
        def _():
            pl.semaphore_signal(
                barrier,
                inc=1,
                device_id={"section": slot // 4, "dp": z * 4 + slot % 4},
                device_id_type=MESH,
            )

        return carry

    lax.fori_loop(0, NSEC * 4, greet, 0)
    for d in range(1, NZ):
        pl.semaphore_signal(barrier, inc=1, device_id=z_peer(d)[1], device_id_type=MESH)
    pl.semaphore_wait(barrier, NSEC * 4 - 1 + NZ - 1)

    g_own = g_ref[:, pl.ds(pl.multiple_of(dp * FB, FB), FB)]
    g1, g1r = g_own.astype(BF16), g_own
    g_rest = g1r - g1.astype(F32)
    g2 = g_rest.astype(BF16)
    g3 = (g_rest - g2.astype(F32)).astype(BF16)
    row_id = lax.broadcasted_iota(jnp.int32, (R_END - R_G, FB), 0)
    g_rows = jnp.where(
        row_id == 0,
        g1.astype(F32),
        jnp.where(row_id == 1, g2.astype(F32), jnp.where(row_id == 2, g3.astype(F32), 0.0)),
    ).astype(BF16)
    weights[sec, quarter, 0:VW] = o_ref[...]
    weights[sec, quarter, R_V:R_A] = v_ref[...].T
    weights[sec, quarter, R_A:R_B] = a_ref[...]
    up_rows = b_ref[pl.ds(pl.multiple_of(quarter * UPR, UPR), UPR), :]
    for w in range(QW):
        weights[sec, quarter, R_B + w * UPR : R_B + (w + 1) * UPR] = up_rows[
            :, w * FB : (w + 1) * FB
        ]
    weights[sec, quarter, R_G:R_END] = g_rows

    def rows_half(half):
        return pl.ds(pl.multiple_of(half * SPLIT, 16), SPLIT)

    def weight_copy(xx, yy, half, target, send_sem):
        k, q = place(xx, yy, core)
        return pltpu.make_async_remote_copy(
            src_ref=weights.at[k, q, rows_half(half)],
            dst_ref=weights.at[k, q, rows_half(half)],
            send_sem=send_sem,
            recv_sem=weight_recv.at[k * 4 + q, half],
            device_id=target,
            device_id_type=MESH,
        )

    tok_row = pl.multiple_of(sec * TOK, TOK)
    HALF = NZ // 2
    SR = HALF * TOK
    stream, owner = z % 2, z // 2
    my_rows = stream * HALF + owner

    def slot_of(zz):
        return (zz % 2) * HALF + zz // 2

    sends = []
    own_states = pltpu.make_async_copy(
        h_ref.at[pl.ds(tok_row, TOK), pl.ds(pl.multiple_of(z * SLAB, SLAB), SLAB)],
        states.at[0, my_rows],
        h_send.at[0],
    )
    own_states.start()
    for d in range(1, NZ):
        zz, target = z_peer(d)
        copy = pltpu.make_async_remote_copy(
            src_ref=h_ref.at[pl.ds(tok_row, TOK), pl.ds(pl.multiple_of(zz * SLAB, SLAB), SLAB)],
            dst_ref=states.at[0, my_rows],
            send_sem=h_send.at[d],
            recv_sem=h_recv.at[z],
            device_id=target,
            device_id_type=MESH,
        )
        copy.start()
        sends.append(copy)

    def weight_wait(k, q, rows, half):
        pltpu.make_async_copy(
            weights.at[k, q, rows], weights.at[k, q, rows], weight_recv.at[k * 4 + q, half]
        ).wait()

    def after(i, n):
        return lax.rem(i + 1, n)

    def before(i, n):
        return lax.rem(i + n - 1, n)

    y_next, y_prev, x_next, x_prev = after(y, NY), before(y, NY), after(x, NX), before(x, NX)

    def column_copies():
        up, down = device(x, y_next, z, core), device(x, y_prev, z, core)
        return [
            weight_copy(x, y, half, target, own_send.at[i])
            for i, (half, target) in enumerate(((0, up), (1, down), (1, up), (0, down)))
        ]

    def column_relay(half):
        source, target = (y_prev, y_next) if half == 0 else (y_next, y_prev)
        return weight_copy(x, source, half, device(x, target, z, core), own_send.at[4 + half])

    def row_copies(ys):
        right, left = device(x_next, y, z, core), device(x_prev, y, z, core)
        return [
            weight_copy(x, ys, half, target, relay_send.at[ys, i])
            for i, (half, target) in enumerate(((0, right), (1, left), (1, right), (0, left)))
        ]

    def row_relays(ys):
        return [
            weight_copy(x_prev, ys, 0, device(x_next, y, z, core), relay_send.at[ys, 4]),
            weight_copy(x_next, ys, 1, device(x_prev, y, z, core), relay_send.at[ys, 5]),
        ]

    def row_send(ys):
        for copy in row_copies(ys):
            copy.start()

    def column(ys, send_row):
        k, q = place(x, ys, core)
        first = jnp.where(y_next == ys, 1, 0)

        @pl.when(y != ys)
        def _():
            for n in (0, 1):
                half = first if n == 0 else 1 - first
                weight_wait(k, q, rows_half(half), half)
                if n == 0:

                    @pl.when(y_prev == ys)
                    def _():
                        column_relay(0).start()

                    @pl.when(y_next == ys)
                    def _():
                        column_relay(1).start()

        if send_row:
            row_send(ys)

    def row_relay(ys):
        first, second = row_relays(ys)
        k, q = place(x_prev, ys, core)
        weight_wait(k, q, rows_half(0), 0)
        first.start()
        k, q = place(x_next, ys, core)
        weight_wait(k, q, rows_half(1), 1)
        second.start()

    @pl.when(jnp.logical_and(y == 0, NY > 1))
    def _():
        for copy in column_copies():
            copy.start()

    column(0, True)

    @pl.when(y != 0)
    def _():
        for copy in column_copies():
            copy.start()

    row_relay(0)

    whole = pl.ds(0, R_END)

    def core_copy(layer, lo):
        q = lo * 2 + core
        return pltpu.make_async_remote_copy(
            src_ref=weights.at[layer, q],
            dst_ref=weights.at[layer, q],
            send_sem=core_send.at[layer, lo],
            recv_sem=weight_recv.at[layer * 4 + q, 0],
            device_id=device(x, y, z, 1 - core),
            device_id_type=MESH,
        )

    def pass_on(layer):
        for lo in (0, 1):
            xs = (layer % 2) * 2 + lo
            q = lo * 2 + core

            @pl.when(jnp.logical_and(xs != x, xs != x_prev))
            def _():
                weight_wait(layer, q, rows_half(0), 0)

            @pl.when(jnp.logical_and(xs != x, xs != x_next))
            def _():
                weight_wait(layer, q, rows_half(1), 1)

            core_copy(layer, lo).start()

    def take_over(layer):
        for lo in (0, 1):
            weight_wait(layer, lo * 2 + (1 - core), whole, 0)

    def gains(layer, q):
        return jnp.sum(weights[layer, q, R_G : R_G + 16].astype(F32), axis=0, keepdims=True)

    def ups(layer):
        return [
            jnp.concatenate(
                [weights[layer, q, R_B + w * UPR : R_B + (w + 1) * UPR] for q in range(4)], axis=0
            )
            for w in range(QW)
        ]

    def peer(st, d):
        zz = 2 * lax.rem(owner + d, HALF) + st
        return zz, {"section": sec, "dp": zz * 4 + quarter}

    def part_copy(st, step, d, lanes):
        zz, target = peer(st, d)
        return pltpu.make_async_remote_copy(
            src_ref=part.at[st, zz // 2, :, pl.ds(0, lanes)],
            dst_ref=arrived.at[step, z, :, pl.ds(0, lanes)],
            send_sem=part_send.at[st, d],
            recv_sem=part_recv.at[z],
            device_id=target,
            device_id_type=MESH,
        )

    def spread_copy(step, d, lanes):
        target = z_peer(d)[1]
        return pltpu.make_async_remote_copy(
            src_ref=spread.at[step, my_rows, :, pl.ds(0, lanes)],
            dst_ref=spread.at[step, my_rows, :, pl.ds(0, lanes)],
            send_sem=spread_send.at[d],
            recv_sem=spread_recv.at[z],
            device_id=target,
            device_id_type=MESH,
        )

    def exchange_start(st, step, lanes):
        @pl.when(stream != st)
        def _():
            part_copy(st, step, 0, lanes).start()

        for d in range(1, HALF):
            part_copy(st, step, d, lanes).start()

    def exchange_sum(st, step, lanes):
        for d in range(1, NZ):
            zz = lax.rem(z + d, NZ)
            ref = arrived.at[step, zz, :, pl.ds(0, lanes)]
            pltpu.make_async_copy(ref, ref, part_recv.at[zz]).wait()
        total = part[st, owner, :, 0:lanes].astype(F32)
        for d in range(1, NZ):
            total = total + arrived[step, lax.rem(z + d, NZ), :, 0:lanes].astype(F32)
        return total

    def spread_start(step, lanes):
        for d in range(1, NZ):
            spread_copy(step, d, lanes).start()

    def exchange_end(st, step, part_lanes, lanes):
        @pl.when(stream != st)
        def _():
            part_copy(st, step, 0, part_lanes).wait_send()

        for d in range(1, HALF):
            part_copy(st, step, d, part_lanes).wait_send()

        def arrive(d):
            zz = peer(st, d)[0]
            ref = spread.at[step, slot_of(zz), :, pl.ds(0, lanes)]
            pltpu.make_async_copy(ref, ref, spread_recv.at[zz]).wait()

        @pl.when(stream != st)
        def _():
            arrive(0)

        for d in range(1, HALF):
            arrive(d)

        @pl.when(stream == st)
        def _():
            for d in range(1, NZ):
                spread_copy(step, d, lanes).wait_send()

    lane_stream = lax.broadcasted_iota(jnp.int32, (SR, 128), 1)
    lane = lax.broadcasted_iota(jnp.int32, (ROWS, 128), 1)
    lane_own = lax.broadcasted_iota(jnp.int32, (TOK, 128), 1)

    def put_scalar(rank_part, scalar, lanes):
        high, low = two_parts(scalar)
        padded = jnp.concatenate([rank_part, jnp.zeros_like(rank_part)], axis=1)
        return jnp.where(
            lanes == RANK,
            high.astype(F32),
            jnp.where(lanes == RANK + 1, low.astype(F32), padded),
        )

    def get_scalar(tile, lanes):
        return jnp.sum(jnp.where(lanes >= RANK, tile, 0.0), axis=1, keepdims=True)

    pass_on(jnp.int32(0))
    for ys in range(1, NY):
        column(ys, ys == 1)
    own_states.wait()
    for d in range(1, NZ):
        zz = lax.rem(z + d, NZ)
        ref = states.at[0, slot_of(zz)]
        pltpu.make_async_copy(ref, ref, h_recv.at[zz]).wait()

    def rows_of(layer, st, q):
        own_rows = slice(st * HALF, (st + 1) * HALF)
        return states[layer, own_rows, :, q * FB : (q + 1) * FB].reshape(SR, FB)

    def forward_part(st, layer):
        ss = jnp.zeros((SR, 1), F32)
        value = jnp.zeros((SR, VW + RANK), F32)
        for q in range(4):
            xq = rows_of(layer, st, q).astype(F32)
            ss = ss + jnp.sum(xq * xq, axis=1, keepdims=True)
            xg = (xq * gains(layer, q)).astype(BF16)
            value = value + dot_nt(xg, weights[layer, q, R_V:R_B])
        part[st, :, :, 0:VW] = value[:, 0:VW].astype(BF16).reshape(HALF, TOK, VW)
        part[st, :, :, VW:PW] = (
            put_scalar(value[:, VW:], ss, lane_stream).astype(BF16).reshape(HALF, TOK, 128)
        )
        exchange_start(st, layer, PW)

    def forward_own(st, layer):
        @pl.when(stream == st)
        def _():
            total = exchange_sum(st, layer, PW)
            totals[layer] = total
            tail = total[:, VW:PW]
            r = lax.rsqrt(get_scalar(tail, lane_own) / WIDTH + NORM_EPS)
            t = (r * tail[:, 0:RANK]).astype(BF16)
            for w, up in enumerate(ups(layer)):
                cols = slice(w * FB, (w + 1) * FB)
                spread[layer, my_rows, :, cols] = (
                    r * total[:, cols] + ADAPTER_SCALE * dot_nn(t, up)
                ).astype(BF16)
            spread_start(layer, VW)

    def forward_end(st, layer):
        exchange_end(st, layer, PW, VW)
        own_rows = slice(st * HALF, (st + 1) * HALF)
        v = spread[layer, own_rows, :, 0:VW].reshape(SR, VW)
        for q in range(4):
            xq = rows_of(layer, st, q).astype(F32)
            states[layer + 1, own_rows, :, q * FB : (q + 1) * FB] = (
                (xq + dot_nn(v, weights[layer, q, 0:VW])).astype(BF16).reshape(HALF, TOK, FB)
            )

    take_over(jnp.int32(0))
    forward_part(0, jnp.int32(0))

    def forward_step(layer, carry):
        @pl.when(layer > 0)
        def _():
            forward_end(1, layer - 1)

        forward_part(1, layer)

        @pl.when(jnp.logical_and(layer % 2 == 1, (layer + 3) // 2 < NY))
        def _():
            row_send((layer + 3) // 2)

        forward_own(0, layer)
        forward_own(1, layer)

        @pl.when(jnp.logical_and(layer % 2 == 0, layer // 2 + 1 < NY))
        def _():
            row_relay(layer // 2 + 1)

        @pl.when(layer + 1 < NSEC)
        def _():
            pass_on(layer + 1)

        forward_end(0, layer)

        @pl.when(layer + 1 < NSEC)
        def _():
            take_over(layer + 1)
            forward_part(0, layer + 1)

        return carry

    lax.fori_loop(0, NSEC, forward_step, 0)
    forward_end(1, jnp.int32(NSEC - 1))

    slab = pl.ds(pl.multiple_of(z * SLAB, SLAB), SLAB)
    head = lg_ref[:, slab] * sw_ref[:, slab]
    last = states[NSEC].reshape(ROWS, SLAB).astype(F32)
    ss = jnp.sum(last * last, axis=1, keepdims=True)
    inner = jnp.sum(last * head, axis=1, keepdims=True)
    rows = lax.broadcasted_iota(jnp.int32, (ROWS, 128), 0)
    mine = jnp.logical_and(rows >= my_rows * TOK, rows < (my_rows + 1) * TOK)
    token_grad = jnp.where(mine, cg_ref[0, sec * TOK // CANDLEN], 0.0)
    table = jnp.where(
        lane == 0, ss, jnp.where(lane == 1, inner, jnp.where(lane == 2, token_grad, 0.0))
    )
    if ROWS != 128:
        table = jnp.concatenate([table] * (128 // ROWS), axis=0)
    scal[z] = table.T[0:8]

    def scal_copy(d):
        zz, target = z_peer(d)
        return pltpu.make_async_remote_copy(
            src_ref=scal.at[z],
            dst_ref=scal.at[z],
            send_sem=scal_send.at[d],
            recv_sem=scal_recv.at[z],
            device_id=target,
            device_id_type=MESH,
        )

    for d in range(1, NZ):
        copy = scal_copy(d)
        copy.start()
        sends.append(copy)
    for d in range(1, NZ):
        zz = lax.rem(z + d, NZ)
        pltpu.make_async_copy(scal.at[zz], scal.at[zz], scal_recv.at[zz]).wait()
    table = jnp.concatenate([jnp.sum(scal[...], axis=0)] * 16, axis=0).T
    if ROWS != 128:
        table = table[0:ROWS]
    ss = jnp.sum(jnp.where(lane == 0, table, 0.0), axis=1, keepdims=True)
    inner = jnp.sum(jnp.where(lane == 1, table, 0.0), axis=1, keepdims=True)
    token_grad = jnp.sum(jnp.where(lane == 2, table, 0.0), axis=1, keepdims=True)
    factor = lax.rsqrt(ss / WIDTH + NORM_EPS)
    token_grad = token_grad / CANDLEN
    grad[...] = (
        token_grad * factor * head
        - token_grad * factor * factor * factor * inner / WIDTH * last
    ).astype(BF16)

    def grad_copy(layer, q):
        return pltpu.make_async_remote_copy(
            src_ref=grad_out.at[layer, q],
            dst_ref=grad_in.at[my_slot],
            send_sem=grad_send.at[layer, q],
            recv_sem=grad_recv.at[my_slot],
            device_id={"section": layer, "dp": z * 4 + q},
            device_id_type=MESH,
        )

    def backward_part(st, layer):
        value = jnp.zeros((SR, VW), F32)
        for q in range(4):
            value = value + dot_nt(
                grad[st * SR : (st + 1) * SR, q * FB : (q + 1) * FB], weights[layer, q, 0:VW]
            )
        part[st, :, :, 0:VW] = value.astype(BF16).reshape(HALF, TOK, VW)
        exchange_start(st, 2 * NSEC - 1 - layer, VW)

    def backward_own(st, layer):
        step = 2 * NSEC - 1 - layer

        @pl.when(stream == st)
        def _():
            forward_total = totals[layer]
            tail = forward_total[:, VW:PW]
            r = lax.rsqrt(get_scalar(tail, lane_own) / WIDTH + NORM_EPS)
            t = (r * tail[:, 0:RANK]).astype(BF16)
            dv = exchange_sum(st, step, VW).astype(BF16)
            dt32 = jnp.zeros((TOK, RANK), F32)
            for w, up in enumerate(ups(layer)):
                dt32 = dt32 + dot_nt(dv[:, w * FB : (w + 1) * FB], up)
            dt = (ADAPTER_SCALE * dt32).astype(BF16)
            dvf, dtf = dv.astype(F32), dt.astype(F32)
            inner = jnp.sum(dvf * forward_total[:, 0:VW], axis=1, keepdims=True) + jnp.sum(
                dtf * tail[:, 0:RANK], axis=1, keepdims=True
            )
            shrink = r * r * r * inner / WIDTH
            spread[step, my_rows, :, 0:VW] = (r * dvf).astype(BF16)
            spread[step, my_rows, :, VW:PW] = put_scalar(r * dtf, shrink, lane_own).astype(BF16)
            spread_start(step, PW)
            up_sum = (ADAPTER_SCALE * dot_tn(t, dv)).astype(BF16)
            for q in range(4):
                for w in range(QW):
                    grad_out[layer, q, RANK + w * UPR : RANK + (w + 1) * UPR] = up_sum[
                        q * UPR : (q + 1) * UPR, w * FB : (w + 1) * FB
                    ]

    def backward_end(st, layer):
        step = 2 * NSEC - 1 - layer
        exchange_end(st, step, VW, PW)
        both = spread[step, st * HALF : (st + 1) * HALF].reshape(SR, PW)
        scaled = both[:, 0 : VW + RANK]
        shrink = get_scalar(both[:, VW:PW].astype(F32), lane_stream)
        own_rows = slice(st * SR, (st + 1) * SR)

        @pl.when(layer > 0)
        def _():
            for q in range(4):
                cols = slice(q * FB, (q + 1) * FB)
                du = dot_nn(scaled, weights[layer, q, R_V:R_B])
                grad[own_rows, cols] = (
                    grad[own_rows, cols].astype(F32)
                    + du * gains(layer, q)
                    - shrink * rows_of(layer, st, q).astype(F32)
                ).astype(BF16)

    def backward_sums(st, layer):
        step = 2 * NSEC - 1 - layer
        rdt = spread[step, st * HALF : (st + 1) * HALF, :, VW : VW + RANK].reshape(SR, RANK)
        for q in range(4):
            share = dot_tn(rdt, rows_of(layer, st, q)) * gains(layer, q)
            if st == 0:
                down_sums[q] = share
                continue
            grad_out[layer, q, 0:RANK] = (down_sums[q] + share).astype(BF16)
            here = jnp.logical_and(layer == sec, quarter == q)

            @pl.when(jnp.logical_not(here))
            def _():
                grad_copy(layer, q).start()

            @pl.when(here)
            def _():
                grad_in[my_slot] = grad_out[layer, q]

    backward_part(0, jnp.int32(NSEC - 1))

    def backward_step(index, carry):
        layer = NSEC - 1 - index

        @pl.when(index > 0)
        def _():
            backward_end(1, layer + 1)

        backward_part(1, layer)

        @pl.when(index > 0)
        def _():
            backward_sums(1, layer + 1)

        backward_own(0, layer)
        backward_own(1, layer)
        backward_end(0, layer)

        @pl.when(layer > 0)
        def _():
            backward_part(0, layer - 1)

        backward_sums(0, layer)
        return carry

    lax.fori_loop(0, NSEC, backward_step, 0)
    backward_end(1, jnp.int32(0))
    backward_sums(1, jnp.int32(0))

    def collect(slot, carry):
        @pl.when(slot != my_slot)
        def _():
            pltpu.make_async_copy(grad_in.at[slot], grad_in.at[slot], grad_recv.at[slot]).wait()

        return carry

    lax.fori_loop(0, NSEC * 4, collect, 0)
    summed = jnp.sum(grad_in[...].astype(F32), axis=0)
    up_z[z] = summed[RANK:GROWS].astype(BF16)
    for d in range(1, NZ):
        zz, target = z_peer(d)
        copy = pltpu.make_async_remote_copy(
            src_ref=up_z.at[z],
            dst_ref=up_z.at[z],
            send_sem=up_send.at[0, d],
            recv_sem=up_recv.at[0, z],
            device_id=target,
            device_id_type=MESH,
        )
        copy.start()
        sends.append(copy)
    gd_ref[...] = summed[0:RANK]
    for d in range(1, NZ):
        zz = lax.rem(z + d, NZ)
        pltpu.make_async_copy(up_z.at[zz], up_z.at[zz], up_recv.at[0, zz]).wait()
    up_q[quarter] = jnp.sum(up_z[...].astype(F32), axis=0)
    for d in range(1, 4):
        copy = pltpu.make_async_remote_copy(
            src_ref=up_q.at[quarter],
            dst_ref=up_q.at[quarter],
            send_sem=up_send.at[1, d],
            recv_sem=up_recv.at[1, quarter],
            device_id={"section": sec, "dp": z * 4 + lax.rem(quarter + d, 4)},
            device_id_type=MESH,
        )
        copy.start()
        sends.append(copy)
    for d in range(1, 4):
        qq = lax.rem(quarter + d, 4)
        pltpu.make_async_copy(up_q.at[qq], up_q.at[qq], up_recv.at[1, qq]).wait()
    for q in range(4):
        for w in range(QW):
            gu_ref[q * UPR : (q + 1) * UPR, w * FB : (w + 1) * FB] = up_q[
                q, w * UPR : (w + 1) * UPR
            ]

    for copy in sends:
        copy.wait_send()
    if NY > 1:
        for copy in column_copies() + [column_relay(0), column_relay(1)]:
            copy.wait_send()
    for ys in range(NY):
        for copy in row_copies(ys) + row_relays(ys):
            copy.wait_send()

    def drain(layer, carry):
        for lo in (0, 1):
            core_copy(layer, lo).wait_send()
        for q in range(4):

            @pl.when(jnp.logical_not(jnp.logical_and(layer == sec, quarter == q)))
            def _():
                grad_copy(layer, q).wait_send()

        return carry

    lax.fori_loop(0, NSEC, drain, 0)


def per_device(
    block_hidden_input,
    cached_score_gradient,
    value_projection,
    output_projection,
    adapter_down_factor,
    adapter_up_factor,
    input_norm_gain,
    last_norm_gain,
    scoring_head_weight,
):
    nsec = lax.axis_size("section")
    nz = lax.axis_size("dp") // 4
    blocks, cand_len, width = block_hidden_input.shape
    tok = blocks * cand_len // nsec
    fb, vw = value_projection.shape[1:]
    rank = adapter_down_factor.shape[2]
    slab, rows = 4 * fb, nz * tok
    upr, qw = rank // 4, vw // fb
    r_end = -(-(2 * vw + rank + upr * qw + 16) // 32) * 32
    pw = vw + 128
    grows = rank + upr * qw
    cfg = (nsec, nz, tok, fb, vw, rank, width, cand_len)
    vmem = pl.BlockSpec(memory_space=pltpu.VMEM)
    dma = pltpu.SemaphoreType.DMA
    grad_down, grad_up = pl.pallas_call(
        functools.partial(kernel, cfg),
        out_shape=(
            jax.ShapeDtypeStruct((rank, fb), F32),
            jax.ShapeDtypeStruct((rank, vw), F32),
        ),
        in_specs=[pl.BlockSpec(memory_space=pl.ANY)]
        + [vmem] * 7
        + [pl.BlockSpec(memory_space=pltpu.SMEM)],
        out_specs=(vmem, vmem),
        scratch_shapes=[
            pltpu.VMEM((nsec, 4, r_end, fb), BF16),
            pltpu.VMEM((nsec + 1, nz, tok, slab), BF16),
            pltpu.VMEM((rows, slab), BF16),
            pltpu.VMEM((2, nz // 2, tok, pw), BF16),
            pltpu.VMEM((2 * nsec, nz, tok, pw), BF16),
            pltpu.VMEM((2 * nsec, nz, tok, pw), BF16),
            pltpu.VMEM((nsec, tok, pw), F32),
            pltpu.VMEM((4, rank, fb), F32),
            pltpu.VMEM((nz, 8, 128), F32),
            pltpu.VMEM((nsec, 4, grows, fb), BF16),
            pltpu.VMEM((nsec * 4, grows, fb), BF16),
            pltpu.VMEM((nz, upr * qw, fb), BF16),
            pltpu.VMEM((4, upr * qw, fb), F32),
            dma((6,)),
            dma((nsec // 2, 6)),
            dma((nsec, 2)),
            dma((nsec * 4, 2)),
            dma((nz,)),
            dma((nz,)),
            dma((2, nz)),
            dma((nz,)),
            dma((nz,)),
            dma((nz,)),
            dma((nz,)),
            dma((nz,)),
            dma((nsec, 4)),
            dma((nsec * 4,)),
            dma((2, 8)),
            dma((2, 8)),
        ],
        compiler_params=pltpu.CompilerParams(
            collective_id=0, has_side_effects=True, vmem_limit_bytes=56 * 1024 * 1024
        ),
        name="layers",
    )(
        block_hidden_input.reshape(blocks * cand_len, width),
        output_projection[0],
        value_projection[0],
        adapter_down_factor[0].T,
        adapter_up_factor[0],
        input_norm_gain,
        last_norm_gain.reshape(1, width),
        scoring_head_weight.reshape(1, width),
        cached_score_gradient.T,
    )
    return (grad_down.T[None], grad_up[None])


def solution(mesh):
    return jax.shard_map(
        per_device,
        mesh=mesh,
        in_specs=(
            P(None, "dp", None),
            P(None, "dp"),
            P("section", "dp", None),
            P("section", None, "dp"),
            P("section", "dp", None),
            P("section", None, None),
            P("section", None),
            P(),
            P(),
        ),
        out_specs=(P("section", "dp", None), P("section", None, None)),
        check_vma=False,
    )
```

```python
import functools

import jax
import jax.numpy as jnp
from jax import lax
from jax.experimental import pallas as pl
from jax.experimental.pallas import tpu as pltpu
from jax.sharding import PartitionSpec as P

ADAPTER_SCALE = 2.0
NORM_EPS = 1e-05
NX = 4
MESH = pl.DeviceIdType.MESH
F32 = jnp.float32
BF16 = jnp.bfloat16


def dot_nn(a, b):
    return lax.dot_general(a, b, (((1,), (0,)), ((), ())), preferred_element_type=F32)


def dot_nt(a, b):
    return lax.dot_general(a, b, (((1,), (1,)), ((), ())), preferred_element_type=F32)


def dot_tn(a, b):
    return lax.dot_general(a, b, (((0,), (0,)), ((), ())), preferred_element_type=F32)


def two_parts(value):
    high = value.astype(BF16)
    low = (value - high.astype(F32)).astype(BF16)
    return high, low


def kernel(
    cfg,
    h_ref,
    o_ref,
    v_ref,
    a_ref,
    b_ref,
    g_ref,
    lg_ref,
    sw_ref,
    cg_ref,
    gd_ref,
    gu_ref,
    weights,
    states,
    grad,
    part,
    arrived,
    spread,
    totals,
    down_sums,
    scal,
    grad_out,
    grad_in,
    up_z,
    up_q,
    own_send,
    relay_send,
    core_send,
    weight_recv,
    h_send,
    h_recv,
    part_send,
    part_recv,
    spread_send,
    spread_recv,
    scal_send,
    scal_recv,
    grad_send,
    grad_recv,
    up_send,
    up_recv,
):
    NSEC, NZ, TOK, FB, VW, RANK, WIDTH, CANDLEN = cfg
    NY = NSEC // 2
    SLAB = 4 * FB
    ROWS = NZ * TOK
    UPR = RANK // 4
    QW = VW // FB
    R_V, R_A, R_G, R_O = 0, VW, VW + RANK, VW + RANK + 32
    R_B = R_O + VW
    R_END = R_B + UPR * QW
    STARTS, SIZES = (0, R_O), (R_O // 2, (R_END - R_O) // 2)
    PW = VW + 128
    GROWS = RANK + UPR * QW

    sec = lax.axis_index("section")
    dp = lax.axis_index("dp")
    y, x_hi = sec // 2, sec % 2
    z, quarter = dp // 4, dp % 4
    x_lo, core = quarter // 2, quarter % 2
    x = x_hi * 2 + x_lo

    def device(xx, yy, zz, cc):
        return {"section": yy * 2 + xx // 2, "dp": zz * 4 + (xx % 2) * 2 + cc}

    def z_peer(d):
        zz = lax.rem(z + d, NZ)
        return zz, {"section": sec, "dp": zz * 4 + quarter}

    def place(xx, yy, cc):
        return yy * 2 + xx // 2, (xx % 2) * 2 + cc

    barrier = pltpu.get_barrier_semaphore()
    my_slot = sec * 4 + quarter

    def greet(slot, carry):
        @pl.when(slot != my_slot)
        def _():
            pl.semaphore_signal(
                barrier,
                inc=1,
                device_id={"section": slot // 4, "dp": z * 4 + slot % 4},
                device_id_type=MESH,
            )

        return carry

    lax.fori_loop(0, NSEC * 4, greet, 0)
    for d in range(1, NZ):
        pl.semaphore_signal(barrier, inc=1, device_id=z_peer(d)[1], device_id_type=MESH)

    g_own = g_ref[:, pl.ds(pl.multiple_of(dp * FB, FB), FB)]
    g1, g1r = g_own.astype(BF16), g_own
    g_rest = g1r - g1.astype(F32)
    g2 = g_rest.astype(BF16)
    g3 = (g_rest - g2.astype(F32)).astype(BF16)
    row_id = lax.broadcasted_iota(jnp.int32, (R_O - R_G, FB), 0)
    g_rows = jnp.where(
        row_id == 0,
        g1.astype(F32),
        jnp.where(row_id == 1, g2.astype(F32), jnp.where(row_id == 2, g3.astype(F32), 0.0)),
    ).astype(BF16)
    weights[sec, quarter, R_O:R_B] = o_ref[...]
    weights[sec, quarter, R_V:R_A] = v_ref[...].T
    weights[sec, quarter, R_A:R_G] = a_ref[...]
    up_rows = b_ref[pl.ds(pl.multiple_of(quarter * UPR, UPR), UPR), :]
    for w in range(QW):
        weights[sec, quarter, R_B + w * UPR : R_B + (w + 1) * UPR] = up_rows[
            :, w * FB : (w + 1) * FB
        ]
    weights[sec, quarter, R_G:R_O] = g_rows

    pl.semaphore_wait(barrier, NSEC * 4 - 1 + NZ - 1)

    def rows_half(pt, half):
        return pl.ds(pl.multiple_of(STARTS[pt] + half * SIZES[pt], 16), SIZES[pt])

    def weight_copy(xx, yy, pt, half, target, send_sem):
        k, q = place(xx, yy, core)
        return pltpu.make_async_remote_copy(
            src_ref=weights.at[k, q, rows_half(pt, half)],
            dst_ref=weights.at[k, q, rows_half(pt, half)],
            send_sem=send_sem,
            recv_sem=weight_recv.at[k * 4 + q, pt * 2 + half],
            device_id=target,
            device_id_type=MESH,
        )

    tok_row = pl.multiple_of(sec * TOK, TOK)
    HALF = NZ // 2
    SR = HALF * TOK
    stream, owner = z % 2, z // 2
    my_rows = stream * HALF + owner

    def slot_of(zz):
        return (zz % 2) * HALF + zz // 2

    sends = []
    own_states = pltpu.make_async_copy(
        h_ref.at[pl.ds(tok_row, TOK), pl.ds(pl.multiple_of(z * SLAB, SLAB), SLAB)],
        states.at[0, my_rows],
        h_send.at[0],
    )
    own_states.start()
    for d in range(1, NZ):
        zz, target = z_peer(d)
        copy = pltpu.make_async_remote_copy(
            src_ref=h_ref.at[pl.ds(tok_row, TOK), pl.ds(pl.multiple_of(zz * SLAB, SLAB), SLAB)],
            dst_ref=states.at[0, my_rows],
            send_sem=h_send.at[d],
            recv_sem=h_recv.at[z],
            device_id=target,
            device_id_type=MESH,
        )
        copy.start()
        sends.append(copy)

    def weight_wait(k, q, pt, half):
        ref = weights.at[k, q, rows_half(pt, half)]
        pltpu.make_async_copy(ref, ref, weight_recv.at[k * 4 + q, pt * 2 + half]).wait()

    def after(i, n):
        return lax.rem(i + 1, n)

    def before(i, n):
        return lax.rem(i + n - 1, n)

    y_next, y_prev, x_next, x_prev = after(y, NY), before(y, NY), after(x, NX), before(x, NX)

    def column_copies(pt):
        up, down = device(x, y_next, z, core), device(x, y_prev, z, core)
        return [
            weight_copy(x, y, pt, half, target, own_send.at[pt, i])
            for i, (half, target) in enumerate(((0, up), (1, down), (1, up), (0, down)))
        ]

    def column_relay(pt, half):
        source, target = (y_prev, y_next) if half == 0 else (y_next, y_prev)
        target = device(x, target, z, core)
        return weight_copy(x, source, pt, half, target, own_send.at[pt, 4 + half])

    def row_copies(ys, pt):
        right, left = device(x_next, y, z, core), device(x_prev, y, z, core)
        return [
            weight_copy(x, ys, pt, half, target, relay_send.at[ys * 2 + pt, i])
            for i, (half, target) in enumerate(((0, right), (1, left), (1, right), (0, left)))
        ]

    def row_relay_copy(ys, pt, half):
        source, target = (x_prev, x_next) if half == 0 else (x_next, x_prev)
        target = device(target, y, z, core)
        return weight_copy(source, ys, pt, half, target, relay_send.at[ys * 2 + pt, 4 + half])

    def row_send(ys, pt):
        for copy in row_copies(ys, pt):
            copy.start()

    def column(ys, pt):
        k, q = place(x, ys, core)
        first = jnp.where(y_next == ys, 1, 0)

        @pl.when(y != ys)
        def _():
            weight_wait(k, q, pt, first)

            @pl.when(y_prev == ys)
            def _():
                column_relay(pt, 0).start()

            @pl.when(y_next == ys)
            def _():
                column_relay(pt, 1).start()

            weight_wait(k, q, pt, 1 - first)

    def row_relay(ys, pt):
        for half, source in ((0, x_prev), (1, x_next)):
            k, q = place(source, ys, core)
            weight_wait(k, q, pt, half)
            row_relay_copy(ys, pt, half).start()

    def core_copy(layer, lo, pt):
        q = lo * 2 + core
        rows = pl.ds(STARTS[pt], 2 * SIZES[pt])
        return pltpu.make_async_remote_copy(
            src_ref=weights.at[layer, q, rows],
            dst_ref=weights.at[layer, q, rows],
            send_sem=core_send.at[layer, lo * 2 + pt],
            recv_sem=weight_recv.at[layer * 4 + q, pt * 2],
            device_id=device(x, y, z, 1 - core),
            device_id_type=MESH,
        )

    def pass_on(layer, pt):
        for lo in (0, 1):
            xs = (layer % 2) * 2 + lo
            q = lo * 2 + core

            @pl.when(jnp.logical_and(xs != x, xs != x_prev))
            def _():
                weight_wait(layer, q, pt, 0)

            @pl.when(jnp.logical_and(xs != x, xs != x_next))
            def _():
                weight_wait(layer, q, pt, 1)

            core_copy(layer, lo, pt).start()

    def take_over(layer, pt):
        for lo in (0, 1):
            q = lo * 2 + (1 - core)
            ref = weights.at[layer, q, pl.ds(STARTS[pt], 2 * SIZES[pt])]
            pltpu.make_async_copy(ref, ref, weight_recv.at[layer * 4 + q, pt * 2]).wait()

    @pl.when(jnp.logical_and(y == 0, NY > 1))
    def _():
        for copy in column_copies(0) + column_copies(1):
            copy.start()

    for pt in (0, 1):
        column(0, pt)
        row_send(0, pt)

    @pl.when(y != 0)
    def _():
        for copy in column_copies(0) + column_copies(1):
            copy.start()

    row_relay(0, 0)

    def gains(layer, q):
        return jnp.sum(weights[layer, q, R_G : R_G + 16].astype(F32), axis=0, keepdims=True)

    def ups(layer):
        return [
            jnp.concatenate(
                [weights[layer, q, R_B + w * UPR : R_B + (w + 1) * UPR] for q in range(4)], axis=0
            )
            for w in range(QW)
        ]

    def peer(st, d):
        zz = 2 * lax.rem(owner + d, HALF) + st
        return zz, {"section": sec, "dp": zz * 4 + quarter}

    def part_copy(st, step, d, lanes):
        zz, target = peer(st, d)
        return pltpu.make_async_remote_copy(
            src_ref=part.at[st, zz // 2, :, pl.ds(0, lanes)],
            dst_ref=arrived.at[step, z, :, pl.ds(0, lanes)],
            send_sem=part_send.at[st, d],
            recv_sem=part_recv.at[z],
            device_id=target,
            device_id_type=MESH,
        )

    def spread_copy(step, d, lanes):
        target = z_peer(d)[1]
        return pltpu.make_async_remote_copy(
            src_ref=spread.at[step, my_rows, :, pl.ds(0, lanes)],
            dst_ref=spread.at[step, my_rows, :, pl.ds(0, lanes)],
            send_sem=spread_send.at[d],
            recv_sem=spread_recv.at[z],
            device_id=target,
            device_id_type=MESH,
        )

    far_first = sorted(range(1, NZ), key=lambda d: -min(d, NZ - d))
    owners_far_first = sorted(range(1, HALF), key=lambda d: -min(d, HALF - d))

    def exchange_start(st, step, lanes):
        for d in owners_far_first:
            part_copy(st, step, d, lanes).start()

        @pl.when(stream != st)
        def _():
            part_copy(st, step, 0, lanes).start()

    def exchange_sum(st, step, lanes):
        for d in range(1, NZ):
            zz = lax.rem(z + d, NZ)
            ref = arrived.at[step, zz, :, pl.ds(0, lanes)]
            pltpu.make_async_copy(ref, ref, part_recv.at[zz]).wait()
        total = part[st, owner, :, 0:lanes].astype(F32)
        for d in range(1, NZ):
            total = total + arrived[step, lax.rem(z + d, NZ), :, 0:lanes].astype(F32)
        return total

    def spread_start(step, lanes):
        for d in far_first:
            spread_copy(step, d, lanes).start()

    def exchange_end(st, step, part_lanes, lanes):
        @pl.when(stream != st)
        def _():
            part_copy(st, step, 0, part_lanes).wait_send()

        for d in range(1, HALF):
            part_copy(st, step, d, part_lanes).wait_send()

        def arrive(d):
            zz = peer(st, d)[0]
            ref = spread.at[step, slot_of(zz), :, pl.ds(0, lanes)]
            pltpu.make_async_copy(ref, ref, spread_recv.at[zz]).wait()

        @pl.when(stream != st)
        def _():
            arrive(0)

        for d in range(1, HALF):
            arrive(d)

        @pl.when(stream == st)
        def _():
            for d in range(1, NZ):
                spread_copy(step, d, lanes).wait_send()

    lane_stream = lax.broadcasted_iota(jnp.int32, (SR, 128), 1)
    lane_own = lax.broadcasted_iota(jnp.int32, (TOK, 128), 1)

    def put_scalar(rank_part, scalar, lanes):
        high, low = two_parts(scalar)
        padded = jnp.concatenate([rank_part, jnp.zeros_like(rank_part)], axis=1)
        return jnp.where(
            lanes == RANK,
            high.astype(F32),
            jnp.where(lanes == RANK + 1, low.astype(F32), padded),
        )

    def get_scalar(tile, lanes):
        return jnp.sum(jnp.where(lanes >= RANK, tile, 0.0), axis=1, keepdims=True)

    pass_on(jnp.int32(0), 0)
    own_states.wait()
    for d in range(1, NZ):
        zz = lax.rem(z + d, NZ)
        ref = states.at[0, slot_of(zz)]
        pltpu.make_async_copy(ref, ref, h_recv.at[zz]).wait()

    def rows_of(layer, st, q):
        own_rows = slice(st * HALF, (st + 1) * HALF)
        return states[layer, own_rows, :, q * FB : (q + 1) * FB].reshape(SR, FB)

    def forward_part(st, layer):
        ss = jnp.zeros((SR, 1), F32)
        value = jnp.zeros((SR, VW + RANK), F32)
        for q in range(4):
            xq = rows_of(layer, st, q).astype(F32)
            ss = ss + jnp.sum(xq * xq, axis=1, keepdims=True)
            xg = (xq * gains(layer, q)).astype(BF16)
            value = value + dot_nt(xg, weights[layer, q, R_V:R_G])
        part[st, :, :, 0:VW] = value[:, 0:VW].astype(BF16).reshape(HALF, TOK, VW)
        part[st, :, :, VW:PW] = (
            put_scalar(value[:, VW:], ss, lane_stream).astype(BF16).reshape(HALF, TOK, 128)
        )
        exchange_start(st, layer, PW)

    def forward_own(st, layer):
        @pl.when(stream == st)
        def _():
            up_factor = ups(layer)
            total = exchange_sum(st, layer, PW)
            totals[layer] = total
            tail = total[:, VW:PW]
            r = lax.rsqrt(get_scalar(tail, lane_own) / WIDTH + NORM_EPS)
            t = (r * tail[:, 0:RANK]).astype(BF16)
            for w, up in enumerate(up_factor):
                cols = slice(w * FB, (w + 1) * FB)
                spread[layer, my_rows, :, cols] = (
                    r * total[:, cols] + ADAPTER_SCALE * dot_nn(t, up)
                ).astype(BF16)
            spread_start(layer, VW)

    def forward_end(st, layer):
        exchange_end(st, layer, PW, VW)
        own_rows = slice(st * HALF, (st + 1) * HALF)
        v = spread[layer, own_rows, :, 0:VW].reshape(SR, VW)
        for q in range(4):
            xq = rows_of(layer, st, q).astype(F32)
            states[layer + 1, own_rows, :, q * FB : (q + 1) * FB] = (
                (xq + dot_nn(v, weights[layer, q, R_O:R_B])).astype(BF16).reshape(HALF, TOK, FB)
            )

    take_over(jnp.int32(0), 0)
    forward_part(0, jnp.int32(0))
    row_relay(0, 1)
    for ys in range(1, NY):
        for pt in (0, 1):
            column(ys, pt)
            if ys == 1:
                row_send(ys, pt)

    def forward_step(layer, carry):
        @pl.when(layer > 0)
        def _():
            forward_end(1, layer - 1)

        forward_part(1, layer)

        pass_on(layer, 1)

        @pl.when(jnp.logical_and(layer % 2 == 1, (layer + 3) // 2 < NY))
        def _():
            for pt in (0, 1):
                row_send((layer + 3) // 2, pt)

        take_over(layer, 1)
        forward_own(0, layer)
        forward_own(1, layer)

        @pl.when(jnp.logical_and(layer % 2 == 0, layer // 2 + 1 < NY))
        def _():
            for pt in (0, 1):
                row_relay(layer // 2 + 1, pt)

        @pl.when(layer + 1 < NSEC)
        def _():
            pass_on(layer + 1, 0)

        forward_end(0, layer)

        @pl.when(layer + 1 < NSEC)
        def _():
            take_over(layer + 1, 0)
            forward_part(0, layer + 1)

        return carry

    slab = pl.ds(pl.multiple_of(z * SLAB, SLAB), SLAB)

    def scal_copy(st, d):
        return pltpu.make_async_remote_copy(
            src_ref=scal.at[st, z],
            dst_ref=scal.at[st, z],
            send_sem=scal_send.at[st, d],
            recv_sem=scal_recv.at[st, z],
            device_id=z_peer(d)[1],
            device_id_type=MESH,
        )

    def last_rows(st):
        rows = states[NSEC, st * HALF : (st + 1) * HALF]
        return rows.reshape(SR, SLAB).astype(F32), lg_ref[:, slab] * sw_ref[:, slab]

    def seed_start(st):
        last, head = last_rows(st)
        ss = jnp.sum(last * last, axis=1, keepdims=True)
        inner = jnp.sum(last * head, axis=1, keepdims=True)
        rows = lax.broadcasted_iota(jnp.int32, (SR, 128), 0)
        mine = jnp.logical_and(
            stream == st, jnp.logical_and(rows >= owner * TOK, rows < (owner + 1) * TOK)
        )
        token_grad = jnp.where(mine, cg_ref[0, sec * TOK // CANDLEN], 0.0)
        table = jnp.where(
            lane_stream == 0,
            ss,
            jnp.where(lane_stream == 1, inner, jnp.where(lane_stream == 2, token_grad, 0.0)),
        )
        scal[st, z] = jnp.concatenate([table] * (128 // SR), axis=0).T[0:8]
        for d in far_first:
            copy = scal_copy(st, d)
            copy.start()
            sends.append(copy)

    def seed_end(st):
        for d in range(1, NZ):
            zz = lax.rem(z + d, NZ)
            ref = scal.at[st, zz]
            pltpu.make_async_copy(ref, ref, scal_recv.at[st, zz]).wait()
        table = jnp.concatenate([jnp.sum(scal[st], axis=0)] * 16, axis=0).T[0:SR]
        ss, inner, token_grad = (
            jnp.sum(jnp.where(lane_stream == i, table, 0.0), axis=1, keepdims=True)
            for i in range(3)
        )
        last, head = last_rows(st)
        factor = lax.rsqrt(ss / WIDTH + NORM_EPS)
        token_grad = token_grad / CANDLEN
        grad[st * SR : (st + 1) * SR] = (
            token_grad * factor * head
            - token_grad * factor * factor * factor * inner / WIDTH * last
        ).astype(BF16)

    lax.fori_loop(0, NSEC, forward_step, 0)
    seed_start(0)
    forward_end(1, jnp.int32(NSEC - 1))
    seed_start(1)
    seed_end(0)

    grad_rows = (pl.ds(0, RANK), pl.ds(RANK, GROWS - RANK))

    def grad_copy(layer, q, pt):
        return pltpu.make_async_remote_copy(
            src_ref=grad_out.at[layer, q, grad_rows[pt]],
            dst_ref=grad_in.at[my_slot, grad_rows[pt]],
            send_sem=grad_send.at[layer, q * 2 + pt],
            recv_sem=grad_recv.at[my_slot, pt],
            device_id={"section": layer, "dp": z * 4 + q},
            device_id_type=MESH,
        )

    def grad_leave(layer, q, pt):
        here = jnp.logical_and(layer == sec, quarter == q)

        @pl.when(jnp.logical_not(here))
        def _():
            grad_copy(layer, q, pt).start()

        @pl.when(here)
        def _():
            grad_in[my_slot, grad_rows[pt]] = grad_out[layer, q, grad_rows[pt]]

    def backward_part(st, layer):
        value = jnp.zeros((SR, VW), F32)
        for q in range(4):
            value = value + dot_nt(
                grad[st * SR : (st + 1) * SR, q * FB : (q + 1) * FB], weights[layer, q, R_O:R_B]
            )
        part[st, :, :, 0:VW] = value.astype(BF16).reshape(HALF, TOK, VW)
        exchange_start(st, 2 * NSEC - 1 - layer, VW)

    def backward_own(st, layer):
        step = 2 * NSEC - 1 - layer

        @pl.when(stream == st)
        def _():
            forward_total = totals[layer]
            tail = forward_total[:, VW:PW]
            r = lax.rsqrt(get_scalar(tail, lane_own) / WIDTH + NORM_EPS)
            t = (r * tail[:, 0:RANK]).astype(BF16)
            up_factor = ups(layer)
            dv = exchange_sum(st, step, VW).astype(BF16)
            dt32 = jnp.zeros((TOK, RANK), F32)
            for w, up in enumerate(up_factor):
                dt32 = dt32 + dot_nt(dv[:, w * FB : (w + 1) * FB], up)
            dt = (ADAPTER_SCALE * dt32).astype(BF16)
            dvf, dtf = dv.astype(F32), dt.astype(F32)
            inner = jnp.sum(dvf * forward_total[:, 0:VW], axis=1, keepdims=True) + jnp.sum(
                dtf * tail[:, 0:RANK], axis=1, keepdims=True
            )
            shrink = r * r * r * inner / WIDTH
            spread[step, my_rows, :, 0:VW] = (r * dvf).astype(BF16)
            spread[step, my_rows, :, VW:PW] = put_scalar(r * dtf, shrink, lane_own).astype(BF16)
            spread_start(step, PW)
            up_sum = (ADAPTER_SCALE * dot_tn(t, dv)).astype(BF16)
            for q in range(4):
                for w in range(QW):
                    grad_out[layer, q, RANK + w * UPR : RANK + (w + 1) * UPR] = up_sum[
                        q * UPR : (q + 1) * UPR, w * FB : (w + 1) * FB
                    ]
                grad_leave(layer, q, 1)

    def backward_end(st, layer):
        step = 2 * NSEC - 1 - layer
        exchange_end(st, step, VW, PW)
        both = spread[step, st * HALF : (st + 1) * HALF].reshape(SR, PW)
        scaled = both[:, 0 : VW + RANK]
        shrink = get_scalar(both[:, VW:PW].astype(F32), lane_stream)
        own_rows = slice(st * SR, (st + 1) * SR)

        @pl.when(layer > 0)
        def _():
            for q in range(4):
                cols = slice(q * FB, (q + 1) * FB)
                du = dot_nn(scaled, weights[layer, q, R_V:R_G])
                grad[own_rows, cols] = (
                    grad[own_rows, cols].astype(F32)
                    + du * gains(layer, q)
                    - shrink * rows_of(layer, st, q).astype(F32)
                ).astype(BF16)

    def backward_sums(st, layer):
        step = 2 * NSEC - 1 - layer
        rdt = spread[step, st * HALF : (st + 1) * HALF, :, VW : VW + RANK].reshape(SR, RANK)
        for q in range(4):
            share = dot_tn(rdt, rows_of(layer, st, q)) * gains(layer, q)
            if st == 0:
                down_sums[q] = share
                continue
            grad_out[layer, q, 0:RANK] = (down_sums[q] + share).astype(BF16)
            grad_leave(layer, q, 0)

    backward_part(0, jnp.int32(NSEC - 1))
    seed_end(1)

    def backward_step(index, carry):
        layer = NSEC - 1 - index

        @pl.when(index > 0)
        def _():
            backward_end(1, layer + 1)

        backward_part(1, layer)

        @pl.when(index > 0)
        def _():
            backward_sums(1, layer + 1)

        backward_own(0, layer)
        backward_own(1, layer)
        backward_end(0, layer)

        @pl.when(layer > 0)
        def _():
            backward_part(0, layer - 1)

        backward_sums(0, layer)
        return carry

    lax.fori_loop(0, NSEC, backward_step, 0)
    backward_end(1, jnp.int32(0))
    backward_sums(1, jnp.int32(0))

    def collect(pt):
        def wait_slot(slot, carry):
            @pl.when(slot != my_slot)
            def _():
                ref = grad_in.at[slot, grad_rows[pt]]
                pltpu.make_async_copy(ref, ref, grad_recv.at[slot, pt]).wait()

            return carry

        lax.fori_loop(0, NSEC * 4, wait_slot, 0)
        return jnp.sum(grad_in[:, grad_rows[pt]].astype(F32), axis=0)

    up_z[z] = collect(1).astype(BF16)
    for d in far_first:
        zz, target = z_peer(d)
        copy = pltpu.make_async_remote_copy(
            src_ref=up_z.at[z],
            dst_ref=up_z.at[z],
            send_sem=up_send.at[0, d],
            recv_sem=up_recv.at[0, z],
            device_id=target,
            device_id_type=MESH,
        )
        copy.start()
        sends.append(copy)
    for d in range(1, NZ):
        zz = lax.rem(z + d, NZ)
        pltpu.make_async_copy(up_z.at[zz], up_z.at[zz], up_recv.at[0, zz]).wait()
    up_q[quarter] = jnp.sum(up_z[...].astype(F32), axis=0)
    for d in range(1, 4):
        copy = pltpu.make_async_remote_copy(
            src_ref=up_q.at[quarter],
            dst_ref=up_q.at[quarter],
            send_sem=up_send.at[1, d],
            recv_sem=up_recv.at[1, quarter],
            device_id={"section": sec, "dp": z * 4 + lax.rem(quarter + d, 4)},
            device_id_type=MESH,
        )
        copy.start()
        sends.append(copy)
    gd_ref[...] = collect(0)
    for d in range(1, 4):
        qq = lax.rem(quarter + d, 4)
        pltpu.make_async_copy(up_q.at[qq], up_q.at[qq], up_recv.at[1, qq]).wait()
    for q in range(4):
        for w in range(QW):
            gu_ref[q * UPR : (q + 1) * UPR, w * FB : (w + 1) * FB] = up_q[
                q, w * UPR : (w + 1) * UPR
            ]

    for copy in sends:
        copy.wait_send()
    for pt in (0, 1):
        if NY > 1:
            for copy in column_copies(pt) + [column_relay(pt, 0), column_relay(pt, 1)]:
                copy.wait_send()
        for ys in range(NY):
            for copy in row_copies(ys, pt) + [row_relay_copy(ys, pt, half) for half in (0, 1)]:
                copy.wait_send()

    def drain(layer, carry):
        for lo in (0, 1):
            for pt in (0, 1):
                core_copy(layer, lo, pt).wait_send()
        for q in range(4):

            @pl.when(jnp.logical_not(jnp.logical_and(layer == sec, quarter == q)))
            def _():
                for pt in (0, 1):
                    grad_copy(layer, q, pt).wait_send()

        return carry

    lax.fori_loop(0, NSEC, drain, 0)


def per_device(
    block_hidden_input,
    cached_score_gradient,
    value_projection,
    output_projection,
    adapter_down_factor,
    adapter_up_factor,
    input_norm_gain,
    last_norm_gain,
    scoring_head_weight,
):
    nsec = lax.axis_size("section")
    nz = lax.axis_size("dp") // 4
    blocks, cand_len, width = block_hidden_input.shape
    tok = blocks * cand_len // nsec
    fb, vw = value_projection.shape[1:]
    rank = adapter_down_factor.shape[2]
    slab, rows = 4 * fb, nz * tok
    upr, qw = rank // 4, vw // fb
    r_end = 2 * vw + rank + upr * qw + 32
    pw = vw + 128
    grows = rank + upr * qw
    cfg = (nsec, nz, tok, fb, vw, rank, width, cand_len)
    vmem = pl.BlockSpec(memory_space=pltpu.VMEM)
    dma = pltpu.SemaphoreType.DMA
    grad_down, grad_up = pl.pallas_call(
        functools.partial(kernel, cfg),
        out_shape=(
            jax.ShapeDtypeStruct((rank, fb), F32),
            jax.ShapeDtypeStruct((rank, vw), F32),
        ),
        in_specs=[pl.BlockSpec(memory_space=pl.ANY)]
        + [vmem] * 7
        + [pl.BlockSpec(memory_space=pltpu.SMEM)],
        out_specs=(vmem, vmem),
        scratch_shapes=[
            pltpu.VMEM((nsec, 4, r_end, fb), BF16),
            pltpu.VMEM((nsec + 1, nz, tok, slab), BF16),
            pltpu.VMEM((rows, slab), BF16),
            pltpu.VMEM((2, nz // 2, tok, pw), BF16),
            pltpu.VMEM((2 * nsec, nz, tok, pw), BF16),
            pltpu.VMEM((2 * nsec, nz, tok, pw), BF16),
            pltpu.VMEM((nsec, tok, pw), F32),
            pltpu.VMEM((4, rank, fb), F32),
            pltpu.VMEM((2, nz, 8, 128), F32),
            pltpu.VMEM((nsec, 4, grows, fb), BF16),
            pltpu.VMEM((nsec * 4, grows, fb), BF16),
            pltpu.VMEM((nz, upr * qw, fb), BF16),
            pltpu.VMEM((4, upr * qw, fb), F32),
            dma((2, 6)),
            dma((nsec, 6)),
            dma((nsec, 4)),
            dma((nsec * 4, 4)),
            dma((nz,)),
            dma((nz,)),
            dma((2, nz)),
            dma((nz,)),
            dma((nz,)),
            dma((nz,)),
            dma((2, nz)),
            dma((2, nz)),
            dma((nsec, 8)),
            dma((nsec * 4, 2)),
            dma((2, 8)),
            dma((2, 8)),
        ],
        compiler_params=pltpu.CompilerParams(
            collective_id=0, has_side_effects=True, vmem_limit_bytes=56 * 1024 * 1024
        ),
        name="layers",
    )(
        block_hidden_input.reshape(blocks * cand_len, width),
        output_projection[0],
        value_projection[0],
        adapter_down_factor[0].T,
        adapter_up_factor[0],
        input_norm_gain,
        last_norm_gain.reshape(1, width),
        scoring_head_weight.reshape(1, width),
        cached_score_gradient.T,
    )
    return (grad_down.T[None], grad_up[None])


def solution(mesh):
    return jax.shard_map(
        per_device,
        mesh=mesh,
        in_specs=(
            P(None, "dp", None),
            P(None, "dp"),
            P("section", "dp", None),
            P("section", None, "dp"),
            P("section", "dp", None),
            P("section", None, None),
            P("section", None),
            P(),
            P(),
        ),
        out_specs=(P("section", "dp", None), P("section", None, None)),
        check_vma=False,
    )
```

```python
import functools

import jax
import jax.numpy as jnp
from jax import lax
from jax.experimental import pallas as pl
from jax.experimental.pallas import tpu as pltpu
from jax.sharding import PartitionSpec as P

ADAPTER_SCALE = 2.0
NORM_EPS = 1e-05
NX = 4
MESH = pl.DeviceIdType.MESH
F32 = jnp.float32
BF16 = jnp.bfloat16


def dot_nn(a, b):
    return lax.dot_general(a, b, (((1,), (0,)), ((), ())), preferred_element_type=F32)


def dot_nt(a, b):
    return lax.dot_general(a, b, (((1,), (1,)), ((), ())), preferred_element_type=F32)


def dot_tn(a, b):
    return lax.dot_general(a, b, (((0,), (0,)), ((), ())), preferred_element_type=F32)


def two_parts(value):
    high = value.astype(BF16)
    low = (value - high.astype(F32)).astype(BF16)
    return high, low


def kernel(
    cfg,
    h_ref,
    o_ref,
    v_ref,
    a_ref,
    b_ref,
    g_ref,
    lg_ref,
    sw_ref,
    cg_ref,
    gd_ref,
    gu_ref,
    weights,
    states,
    grad,
    part,
    arrived,
    spread,
    totals,
    down_sums,
    scal,
    grad_out,
    grad_in,
    up_z,
    up_q,
    own_send,
    relay_send,
    wide_send,
    core_send,
    weight_recv,
    h_send,
    h_recv,
    part_send,
    part_recv,
    spread_send,
    spread_recv,
    scal_send,
    scal_recv,
    grad_send,
    grad_recv,
    up_send,
    up_recv,
):
    NSEC, NZ, TOK, FB, VW, RANK, WIDTH, CANDLEN = cfg
    NY = NSEC // 2
    SLAB = 4 * FB
    ROWS = NZ * TOK
    UPR = RANK // 4
    QW = VW // FB
    R_V, R_A, R_G, R_O = 0, VW, VW + RANK, VW + RANK + 32
    R_B = R_O + VW
    R_END = R_B + UPR * QW
    STARTS, SIZES = (0, R_O), (R_O // 2, (R_END - R_O) // 2)
    PW = VW + 128
    GROWS = RANK + UPR * QW

    sec = lax.axis_index("section")
    dp = lax.axis_index("dp")
    y, x_hi = sec // 2, sec % 2
    z, quarter = dp // 4, dp % 4
    x_lo, core = quarter // 2, quarter % 2
    x = x_hi * 2 + x_lo

    def device(xx, yy, zz, cc):
        return {"section": yy * 2 + xx // 2, "dp": zz * 4 + (xx % 2) * 2 + cc}

    def z_peer(d):
        zz = lax.rem(z + d, NZ)
        return zz, {"section": sec, "dp": zz * 4 + quarter}

    def place(xx, yy, cc):
        return yy * 2 + xx // 2, (xx % 2) * 2 + cc

    barrier = pltpu.get_barrier_semaphore()
    my_slot = sec * 4 + quarter

    def greet(slot, carry):
        @pl.when(slot != my_slot)
        def _():
            pl.semaphore_signal(
                barrier,
                inc=1,
                device_id={"section": slot // 4, "dp": z * 4 + slot % 4},
                device_id_type=MESH,
            )

        return carry

    lax.fori_loop(0, NSEC * 4, greet, 0)
    for d in range(1, NZ):
        pl.semaphore_signal(barrier, inc=1, device_id=z_peer(d)[1], device_id_type=MESH)

    g_own = g_ref[:, pl.ds(pl.multiple_of(dp * FB, FB), FB)]
    g1, g1r = g_own.astype(BF16), g_own
    g_rest = g1r - g1.astype(F32)
    g2 = g_rest.astype(BF16)
    g3 = (g_rest - g2.astype(F32)).astype(BF16)
    row_id = lax.broadcasted_iota(jnp.int32, (R_O - R_G, FB), 0)
    g_rows = jnp.where(
        row_id == 0,
        g1.astype(F32),
        jnp.where(row_id == 1, g2.astype(F32), jnp.where(row_id == 2, g3.astype(F32), 0.0)),
    ).astype(BF16)
    weights[sec, quarter, R_O:R_B] = o_ref[...]
    weights[sec, quarter, R_V:R_A] = v_ref[...].T
    weights[sec, quarter, R_A:R_G] = a_ref[...]
    up_rows = b_ref[pl.ds(pl.multiple_of(quarter * UPR, UPR), UPR), :]
    for w in range(QW):
        weights[sec, quarter, R_B + w * UPR : R_B + (w + 1) * UPR] = up_rows[
            :, w * FB : (w + 1) * FB
        ]
    weights[sec, quarter, R_G:R_O] = g_rows

    pl.semaphore_wait(barrier, NSEC * 4 - 1 + NZ - 1)

    def rows_half(pt, half):
        return pl.ds(pl.multiple_of(STARTS[pt] + half * SIZES[pt], 16), SIZES[pt])

    def weight_copy(xx, yy, pt, half, target, send_sem):
        k, q = place(xx, yy, core)
        return pltpu.make_async_remote_copy(
            src_ref=weights.at[k, q, rows_half(pt, half)],
            dst_ref=weights.at[k, q, rows_half(pt, half)],
            send_sem=send_sem,
            recv_sem=weight_recv.at[k * 4 + q, pt * 2 + half],
            device_id=target,
            device_id_type=MESH,
        )

    tok_row = pl.multiple_of(sec * TOK, TOK)
    HALF = NZ // 2
    SR = HALF * TOK
    stream, owner = z % 2, z // 2
    my_rows = stream * HALF + owner

    def slot_of(zz):
        return (zz % 2) * HALF + zz // 2

    sends = []
    own_states = pltpu.make_async_copy(
        h_ref.at[pl.ds(tok_row, TOK), pl.ds(pl.multiple_of(z * SLAB, SLAB), SLAB)],
        states.at[0, my_rows],
        h_send.at[0],
    )
    own_states.start()
    for d in range(1, NZ):
        zz, target = z_peer(d)
        copy = pltpu.make_async_remote_copy(
            src_ref=h_ref.at[pl.ds(tok_row, TOK), pl.ds(pl.multiple_of(zz * SLAB, SLAB), SLAB)],
            dst_ref=states.at[0, my_rows],
            send_sem=h_send.at[d],
            recv_sem=h_recv.at[z],
            device_id=target,
            device_id_type=MESH,
        )
        copy.start()
        sends.append(copy)

    def weight_wait(k, q, pt, half):
        ref = weights.at[k, q, rows_half(pt, half)]
        pltpu.make_async_copy(ref, ref, weight_recv.at[k * 4 + q, pt * 2 + half]).wait()

    def after(i, n):
        return lax.rem(i + 1, n)

    def before(i, n):
        return lax.rem(i + n - 1, n)

    y_next, y_prev, x_next, x_prev = after(y, NY), before(y, NY), after(x, NX), before(x, NX)

    def column_copies(pt):
        up, down = device(x, y_next, z, core), device(x, y_prev, z, core)
        return [
            weight_copy(x, y, pt, half, target, own_send.at[pt, i])
            for i, (half, target) in enumerate(((0, up), (1, down), (1, up), (0, down)))
        ]

    def column_relay(pt, half):
        source, target = (y_prev, y_next) if half == 0 else (y_next, y_prev)
        target = device(x, target, z, core)
        return weight_copy(x, source, pt, half, target, own_send.at[pt, 4 + half])

    def row_copies(ys, pt):
        right, left = device(x_next, y, z, core), device(x_prev, y, z, core)
        return [
            weight_copy(x, ys, pt, half, target, relay_send.at[ys * 2 + pt, i])
            for i, (half, target) in enumerate(((0, right), (1, left), (1, right), (0, left)))
        ]

    def row_relay_copy(ys, pt, half):
        source, target = (x_prev, x_next) if half == 0 else (x_next, x_prev)
        target = device(target, y, z, core)
        return weight_copy(source, ys, pt, half, target, relay_send.at[ys * 2 + pt, 4 + half])

    def row_send(ys, pt):
        for copy in row_copies(ys, pt):
            copy.start()

    def column(ys, pt):
        k, q = place(x, ys, core)
        first = jnp.where(y_next == ys, 1, 0)

        @pl.when(y != ys)
        def _():
            weight_wait(k, q, pt, first)

            @pl.when(y_prev == ys)
            def _():
                column_relay(pt, 0).start()

            @pl.when(y_next == ys)
            def _():
                column_relay(pt, 1).start()

            weight_wait(k, q, pt, 1 - first)

    def row_relay(ys, pt):
        for half, source in ((0, x_prev), (1, x_next)):
            k, q = place(source, ys, core)
            weight_wait(k, q, pt, half)
            row_relay_copy(ys, pt, half).start()

    def wide_copies(xs):
        up, down = device(x, y_next, z, core), device(x, y_prev, z, core)
        return [
            weight_copy(xs, y, 1, half, target, wide_send.at[xs, i])
            for i, (half, target) in enumerate(((0, up), (1, down), (1, up), (0, down)))
        ]

    def wide_relay(xs, half):
        source, target = (y_prev, y_next) if half == 0 else (y_next, y_prev)
        target = device(x, target, z, core)
        return weight_copy(xs, source, 1, half, target, wide_send.at[xs, 4 + half])

    def wide_send_all():
        row_relay(y, 1)
        for source, half in ((x_prev, 1), (x_next, 0)):
            k, q = place(source, y, core)
            weight_wait(k, q, 1, half)
        k, q = place(lax.rem(x + 2, NX), y, core)
        for half in (0, 1):
            weight_wait(k, q, 1, half)
        for xs in range(NX):
            for copy in wide_copies(xs):
                copy.start()

    def wide_near(ys):
        for half, source in ((0, y_prev), (1, y_next)):

            @pl.when(source == ys)
            def _():
                for xs in range(NX):
                    k, q = place(xs, ys, core)
                    weight_wait(k, q, 1, half)
                    wide_relay(xs, half).start()

    def wide_rest(ys):
        for half, source in ((0, y_prev), (1, y_next)):

            @pl.when(jnp.logical_and(y != ys, source != ys))
            def _():
                for xs in range(NX):
                    k, q = place(xs, ys, core)
                    weight_wait(k, q, 1, half)

    def core_copy(layer, lo, pt):
        q = lo * 2 + core
        rows = pl.ds(STARTS[pt], 2 * SIZES[pt])
        return pltpu.make_async_remote_copy(
            src_ref=weights.at[layer, q, rows],
            dst_ref=weights.at[layer, q, rows],
            send_sem=core_send.at[layer, lo * 2 + pt],
            recv_sem=weight_recv.at[layer * 4 + q, pt * 2],
            device_id=device(x, y, z, 1 - core),
            device_id_type=MESH,
        )

    def pass_on(layer, pt):
        for lo in (0, 1):
            xs = (layer % 2) * 2 + lo
            q = lo * 2 + core

            narrow = jnp.logical_or(layer < 2, pt == 0)

            @pl.when(jnp.logical_and(narrow, jnp.logical_and(xs != x, xs != x_prev)))
            def _():
                weight_wait(layer, q, pt, 0)

            @pl.when(jnp.logical_and(narrow, jnp.logical_and(xs != x, xs != x_next)))
            def _():
                weight_wait(layer, q, pt, 1)

            core_copy(layer, lo, pt).start()

    def take_over(layer, pt):
        for lo in (0, 1):
            q = lo * 2 + (1 - core)
            ref = weights.at[layer, q, pl.ds(STARTS[pt], 2 * SIZES[pt])]
            pltpu.make_async_copy(ref, ref, weight_recv.at[layer * 4 + q, pt * 2]).wait()

    @pl.when(jnp.logical_and(y == 0, NY > 1))
    def _():
        for copy in column_copies(0) + column_copies(1):
            copy.start()

    for pt in (0, 1):
        column(0, pt)
        row_send(0, pt)

    @pl.when(y != 0)
    def _():
        for copy in column_copies(0):
            copy.start()
        row_send(y, 1)

    row_relay(0, 0)

    def gains(layer, q):
        return jnp.sum(weights[layer, q, R_G : R_G + 16].astype(F32), axis=0, keepdims=True)

    def ups(layer):
        return [
            jnp.concatenate(
                [weights[layer, q, R_B + w * UPR : R_B + (w + 1) * UPR] for q in range(4)], axis=0
            )
            for w in range(QW)
        ]

    def peer(st, d):
        zz = 2 * lax.rem(owner + d, HALF) + st
        return zz, {"section": sec, "dp": zz * 4 + quarter}

    def part_copy(st, step, d, lanes):
        zz, target = peer(st, d)
        return pltpu.make_async_remote_copy(
            src_ref=part.at[st, zz // 2, :, pl.ds(0, lanes)],
            dst_ref=arrived.at[step, z, :, pl.ds(0, lanes)],
            send_sem=part_send.at[st, d],
            recv_sem=part_recv.at[z],
            device_id=target,
            device_id_type=MESH,
        )

    def spread_copy(step, d, lanes):
        target = z_peer(d)[1]
        return pltpu.make_async_remote_copy(
            src_ref=spread.at[step, my_rows, :, pl.ds(0, lanes)],
            dst_ref=spread.at[step, my_rows, :, pl.ds(0, lanes)],
            send_sem=spread_send.at[d],
            recv_sem=spread_recv.at[z],
            device_id=target,
            device_id_type=MESH,
        )

    far_first = sorted(range(1, NZ), key=lambda d: -min(d, NZ - d))
    owners_far_first = sorted(range(1, HALF), key=lambda d: -min(d, HALF - d))

    def exchange_start(st, step, lanes):
        for d in owners_far_first:
            part_copy(st, step, d, lanes).start()

        @pl.when(stream != st)
        def _():
            part_copy(st, step, 0, lanes).start()

    def exchange_sum(st, step, lanes):
        for d in range(1, NZ):
            zz = lax.rem(z + d, NZ)
            ref = arrived.at[step, zz, :, pl.ds(0, lanes)]
            pltpu.make_async_copy(ref, ref, part_recv.at[zz]).wait()
        total = part[st, owner, :, 0:lanes].astype(F32)
        for d in range(1, NZ):
            total = total + arrived[step, lax.rem(z + d, NZ), :, 0:lanes].astype(F32)
        return total

    def spread_start(step, lanes):
        for d in far_first:
            spread_copy(step, d, lanes).start()

    def exchange_end(st, step, part_lanes, lanes):
        @pl.when(stream != st)
        def _():
            part_copy(st, step, 0, part_lanes).wait_send()

        for d in range(1, HALF):
            part_copy(st, step, d, part_lanes).wait_send()

        def arrive(d):
            zz = peer(st, d)[0]
            ref = spread.at[step, slot_of(zz), :, pl.ds(0, lanes)]
            pltpu.make_async_copy(ref, ref, spread_recv.at[zz]).wait()

        @pl.when(stream != st)
        def _():
            arrive(0)

        for d in range(1, HALF):
            arrive(d)

        @pl.when(stream == st)
        def _():
            for d in range(1, NZ):
                spread_copy(step, d, lanes).wait_send()

    lane_stream = lax.broadcasted_iota(jnp.int32, (SR, 128), 1)
    lane_own = lax.broadcasted_iota(jnp.int32, (TOK, 128), 1)

    def put_scalar(rank_part, scalar, lanes):
        high, low = two_parts(scalar)
        padded = jnp.concatenate([rank_part, jnp.zeros_like(rank_part)], axis=1)
        return jnp.where(
            lanes == RANK,
            high.astype(F32),
            jnp.where(lanes == RANK + 1, low.astype(F32), padded),
        )

    def get_scalar(tile, lanes):
        return jnp.sum(jnp.where(lanes >= RANK, tile, 0.0), axis=1, keepdims=True)

    pass_on(jnp.int32(0), 0)
    own_states.wait()
    for d in range(1, NZ):
        zz = lax.rem(z + d, NZ)
        ref = states.at[0, slot_of(zz)]
        pltpu.make_async_copy(ref, ref, h_recv.at[zz]).wait()

    def rows_of(layer, st, q):
        own_rows = slice(st * HALF, (st + 1) * HALF)
        return states[layer, own_rows, :, q * FB : (q + 1) * FB].reshape(SR, FB)

    def forward_part(st, layer):
        ss = jnp.zeros((SR, 1), F32)
        value = jnp.zeros((SR, VW + RANK), F32)
        for q in range(4):
            xq = rows_of(layer, st, q).astype(F32)
            ss = ss + jnp.sum(xq * xq, axis=1, keepdims=True)
            xg = (xq * gains(layer, q)).astype(BF16)
            value = value + dot_nt(xg, weights[layer, q, R_V:R_G])
        part[st, :, :, 0:VW] = value[:, 0:VW].astype(BF16).reshape(HALF, TOK, VW)
        part[st, :, :, VW:PW] = (
            put_scalar(value[:, VW:], ss, lane_stream).astype(BF16).reshape(HALF, TOK, 128)
        )
        exchange_start(st, layer, PW)

    def forward_own(st, layer):
        @pl.when(stream == st)
        def _():
            up_factor = ups(layer)
            total = exchange_sum(st, layer, PW)
            totals[layer] = total
            tail = total[:, VW:PW]
            r = lax.rsqrt(get_scalar(tail, lane_own) / WIDTH + NORM_EPS)
            t = (r * tail[:, 0:RANK]).astype(BF16)
            for w, up in enumerate(up_factor):
                cols = slice(w * FB, (w + 1) * FB)
                spread[layer, my_rows, :, cols] = (
                    r * total[:, cols] + ADAPTER_SCALE * dot_nn(t, up)
                ).astype(BF16)
            spread_start(layer, VW)

    def forward_end(st, layer):
        exchange_end(st, layer, PW, VW)
        own_rows = slice(st * HALF, (st + 1) * HALF)
        v = spread[layer, own_rows, :, 0:VW].reshape(SR, VW)
        for q in range(4):
            xq = rows_of(layer, st, q).astype(F32)
            states[layer + 1, own_rows, :, q * FB : (q + 1) * FB] = (
                (xq + dot_nn(v, weights[layer, q, R_O:R_B])).astype(BF16).reshape(HALF, TOK, FB)
            )

    take_over(jnp.int32(0), 0)
    forward_part(0, jnp.int32(0))
    row_relay(0, 1)
    for ys in range(1, NY):
        column(ys, 0)
        if ys == 1:
            row_send(ys, 0)

    @pl.when(y != 0)
    def _():
        wide_send_all()

    def forward_step(layer, carry):
        @pl.when(layer > 0)
        def _():
            forward_end(1, layer - 1)

        forward_part(1, layer)

        @pl.when(jnp.logical_and(layer % 2 == 0, layer > 0))
        def _():
            wide_rest(layer // 2)

        pass_on(layer, 1)

        @pl.when(jnp.logical_and(layer % 2 == 1, (layer + 3) // 2 < NY))
        def _():
            row_send((layer + 3) // 2, 0)

        take_over(layer, 1)
        forward_own(0, layer)
        forward_own(1, layer)

        @pl.when(jnp.logical_and(layer % 2 == 0, layer // 2 + 1 < NY))
        def _():
            row_relay(layer // 2 + 1, 0)
            wide_near(layer // 2 + 1)

        @pl.when(layer + 1 < NSEC)
        def _():
            pass_on(layer + 1, 0)

        forward_end(0, layer)

        @pl.when(layer + 1 < NSEC)
        def _():
            take_over(layer + 1, 0)
            forward_part(0, layer + 1)

        return carry

    slab = pl.ds(pl.multiple_of(z * SLAB, SLAB), SLAB)

    def scal_copy(st, d):
        return pltpu.make_async_remote_copy(
            src_ref=scal.at[st, z],
            dst_ref=scal.at[st, z],
            send_sem=scal_send.at[st, d],
            recv_sem=scal_recv.at[st, z],
            device_id=z_peer(d)[1],
            device_id_type=MESH,
        )

    def last_rows(st):
        rows = states[NSEC, st * HALF : (st + 1) * HALF]
        return rows.reshape(SR, SLAB).astype(F32), lg_ref[:, slab] * sw_ref[:, slab]

    def seed_start(st):
        last, head = last_rows(st)
        ss = jnp.sum(last * last, axis=1, keepdims=True)
        inner = jnp.sum(last * head, axis=1, keepdims=True)
        rows = lax.broadcasted_iota(jnp.int32, (SR, 128), 0)
        mine = jnp.logical_and(
            stream == st, jnp.logical_and(rows >= owner * TOK, rows < (owner + 1) * TOK)
        )
        token_grad = jnp.where(mine, cg_ref[0, sec * TOK // CANDLEN], 0.0)
        table = jnp.where(
            lane_stream == 0,
            ss,
            jnp.where(lane_stream == 1, inner, jnp.where(lane_stream == 2, token_grad, 0.0)),
        )
        scal[st, z] = jnp.concatenate([table] * (128 // SR), axis=0).T[0:8]
        for d in far_first:
            copy = scal_copy(st, d)
            copy.start()
            sends.append(copy)

    def seed_end(st):
        for d in range(1, NZ):
            zz = lax.rem(z + d, NZ)
            ref = scal.at[st, zz]
            pltpu.make_async_copy(ref, ref, scal_recv.at[st, zz]).wait()
        table = jnp.concatenate([jnp.sum(scal[st], axis=0)] * 16, axis=0).T[0:SR]
        ss, inner, token_grad = (
            jnp.sum(jnp.where(lane_stream == i, table, 0.0), axis=1, keepdims=True)
            for i in range(3)
        )
        last, head = last_rows(st)
        factor = lax.rsqrt(ss / WIDTH + NORM_EPS)
        token_grad = token_grad / CANDLEN
        grad[st * SR : (st + 1) * SR] = (
            token_grad * factor * head
            - token_grad * factor * factor * factor * inner / WIDTH * last
        ).astype(BF16)

    lax.fori_loop(0, NSEC, forward_step, 0)
    seed_start(0)
    forward_end(1, jnp.int32(NSEC - 1))
    seed_start(1)
    seed_end(0)

    grad_rows = (pl.ds(0, RANK), pl.ds(RANK, GROWS - RANK))

    def grad_copy(layer, q, pt):
        return pltpu.make_async_remote_copy(
            src_ref=grad_out.at[layer, q, grad_rows[pt]],
            dst_ref=grad_in.at[my_slot, grad_rows[pt]],
            send_sem=grad_send.at[layer, q * 2 + pt],
            recv_sem=grad_recv.at[my_slot, pt],
            device_id={"section": layer, "dp": z * 4 + q},
            device_id_type=MESH,
        )

    def grad_leave(layer, q, pt):
        here = jnp.logical_and(layer == sec, quarter == q)

        @pl.when(jnp.logical_not(here))
        def _():
            grad_copy(layer, q, pt).start()

        @pl.when(here)
        def _():
            grad_in[my_slot, grad_rows[pt]] = grad_out[layer, q, grad_rows[pt]]

    def backward_part(st, layer):
        value = jnp.zeros((SR, VW), F32)
        for q in range(4):
            value = value + dot_nt(
                grad[st * SR : (st + 1) * SR, q * FB : (q + 1) * FB], weights[layer, q, R_O:R_B]
            )
        part[st, :, :, 0:VW] = value.astype(BF16).reshape(HALF, TOK, VW)
        exchange_start(st, 2 * NSEC - 1 - layer, VW)

    def backward_own(st, layer):
        step = 2 * NSEC - 1 - layer

        @pl.when(stream == st)
        def _():
            forward_total = totals[layer]
            tail = forward_total[:, VW:PW]
            r = lax.rsqrt(get_scalar(tail, lane_own) / WIDTH + NORM_EPS)
            t = (r * tail[:, 0:RANK]).astype(BF16)
            up_factor = ups(layer)
            dv = exchange_sum(st, step, VW).astype(BF16)
            dt32 = jnp.zeros((TOK, RANK), F32)
            for w, up in enumerate(up_factor):
                dt32 = dt32 + dot_nt(dv[:, w * FB : (w + 1) * FB], up)
            dt = (ADAPTER_SCALE * dt32).astype(BF16)
            dvf, dtf = dv.astype(F32), dt.astype(F32)
            inner = jnp.sum(dvf * forward_total[:, 0:VW], axis=1, keepdims=True) + jnp.sum(
                dtf * tail[:, 0:RANK], axis=1, keepdims=True
            )
            shrink = r * r * r * inner / WIDTH
            spread[step, my_rows, :, 0:VW] = (r * dvf).astype(BF16)
            spread[step, my_rows, :, VW:PW] = put_scalar(r * dtf, shrink, lane_own).astype(BF16)
            spread_start(step, PW)
            up_sum = (ADAPTER_SCALE * dot_tn(t, dv)).astype(BF16)
            for q in range(4):
                for w in range(QW):
                    grad_out[layer, q, RANK + w * UPR : RANK + (w + 1) * UPR] = up_sum[
                        q * UPR : (q + 1) * UPR, w * FB : (w + 1) * FB
                    ]
                grad_leave(layer, q, 1)

    def backward_end(st, layer):
        step = 2 * NSEC - 1 - layer
        exchange_end(st, step, VW, PW)
        both = spread[step, st * HALF : (st + 1) * HALF].reshape(SR, PW)
        scaled = both[:, 0 : VW + RANK]
        shrink = get_scalar(both[:, VW:PW].astype(F32), lane_stream)
        own_rows = slice(st * SR, (st + 1) * SR)

        @pl.when(layer > 0)
        def _():
            for q in range(4):
                cols = slice(q * FB, (q + 1) * FB)
                du = dot_nn(scaled, weights[layer, q, R_V:R_G])
                grad[own_rows, cols] = (
                    grad[own_rows, cols].astype(F32)
                    + du * gains(layer, q)
                    - shrink * rows_of(layer, st, q).astype(F32)
                ).astype(BF16)

    def backward_sums(st, layer):
        step = 2 * NSEC - 1 - layer
        rdt = spread[step, st * HALF : (st + 1) * HALF, :, VW : VW + RANK].reshape(SR, RANK)
        for q in range(4):
            share = dot_tn(rdt, rows_of(layer, st, q)) * gains(layer, q)
            if st == 0:
                down_sums[q] = share
                continue
            grad_out[layer, q, 0:RANK] = (down_sums[q] + share).astype(BF16)
            grad_leave(layer, q, 0)

    backward_part(0, jnp.int32(NSEC - 1))
    seed_end(1)

    def backward_step(index, carry):
        layer = NSEC - 1 - index

        @pl.when(index > 0)
        def _():
            backward_end(1, layer + 1)

        backward_part(1, layer)

        @pl.when(index > 0)
        def _():
            backward_sums(1, layer + 1)

        backward_own(0, layer)
        backward_own(1, layer)
        backward_end(0, layer)

        @pl.when(layer > 0)
        def _():
            backward_part(0, layer - 1)

        backward_sums(0, layer)
        return carry

    lax.fori_loop(0, NSEC, backward_step, 0)
    backward_end(1, jnp.int32(0))
    backward_sums(1, jnp.int32(0))

    def collect(pt):
        def wait_slot(slot, carry):
            @pl.when(slot != my_slot)
            def _():
                ref = grad_in.at[slot, grad_rows[pt]]
                pltpu.make_async_copy(ref, ref, grad_recv.at[slot, pt]).wait()

            return carry

        lax.fori_loop(0, NSEC * 4, wait_slot, 0)
        return jnp.sum(grad_in[:, grad_rows[pt]].astype(F32), axis=0)

    up_z[z] = collect(1).astype(BF16)
    for d in far_first:
        zz, target = z_peer(d)
        copy = pltpu.make_async_remote_copy(
            src_ref=up_z.at[z],
            dst_ref=up_z.at[z],
            send_sem=up_send.at[0, d],
            recv_sem=up_recv.at[0, z],
            device_id=target,
            device_id_type=MESH,
        )
        copy.start()
        sends.append(copy)
    for d in range(1, NZ):
        zz = lax.rem(z + d, NZ)
        pltpu.make_async_copy(up_z.at[zz], up_z.at[zz], up_recv.at[0, zz]).wait()
    up_q[quarter] = jnp.sum(up_z[...].astype(F32), axis=0)
    for d in range(1, 4):
        copy = pltpu.make_async_remote_copy(
            src_ref=up_q.at[quarter],
            dst_ref=up_q.at[quarter],
            send_sem=up_send.at[1, d],
            recv_sem=up_recv.at[1, quarter],
            device_id={"section": sec, "dp": z * 4 + lax.rem(quarter + d, 4)},
            device_id_type=MESH,
        )
        copy.start()
        sends.append(copy)
    gd_ref[...] = collect(0)
    for d in range(1, 4):
        qq = lax.rem(quarter + d, 4)
        pltpu.make_async_copy(up_q.at[qq], up_q.at[qq], up_recv.at[1, qq]).wait()
    for q in range(4):
        for w in range(QW):
            gu_ref[q * UPR : (q + 1) * UPR, w * FB : (w + 1) * FB] = up_q[
                q, w * UPR : (w + 1) * UPR
            ]

    for copy in sends:
        copy.wait_send()
    def row_done(ys, pt):
        for copy in row_copies(ys, pt) + [row_relay_copy(ys, pt, half) for half in (0, 1)]:
            copy.wait_send()

    for ys in range(NY):
        row_done(ys, 0)
    row_done(0, 1)
    if NY > 1:
        for copy in column_copies(0) + [column_relay(0, 0), column_relay(0, 1)]:
            copy.wait_send()

        @pl.when(y == 0)
        def _():
            for copy in column_copies(1):
                copy.wait_send()

        @pl.when(y != 0)
        def _():
            row_done(y, 1)
            for xs in range(NX):
                for copy in wide_copies(xs):
                    copy.wait_send()

        for half, source in ((0, y_prev), (1, y_next)):

            @pl.when(source == 0)
            def _():
                column_relay(1, half).wait_send()

            @pl.when(source != 0)
            def _():
                for xs in range(NX):
                    wide_relay(xs, half).wait_send()

    def drain(layer, carry):
        for lo in (0, 1):
            for pt in (0, 1):
                core_copy(layer, lo, pt).wait_send()
        for q in range(4):

            @pl.when(jnp.logical_not(jnp.logical_and(layer == sec, quarter == q)))
            def _():
                for pt in (0, 1):
                    grad_copy(layer, q, pt).wait_send()

        return carry

    lax.fori_loop(0, NSEC, drain, 0)


def per_device(
    block_hidden_input,
    cached_score_gradient,
    value_projection,
    output_projection,
    adapter_down_factor,
    adapter_up_factor,
    input_norm_gain,
    last_norm_gain,
    scoring_head_weight,
):
    nsec = lax.axis_size("section")
    nz = lax.axis_size("dp") // 4
    blocks, cand_len, width = block_hidden_input.shape
    tok = blocks * cand_len // nsec
    fb, vw = value_projection.shape[1:]
    rank = adapter_down_factor.shape[2]
    slab, rows = 4 * fb, nz * tok
    upr, qw = rank // 4, vw // fb
    r_end = 2 * vw + rank + upr * qw + 32
    pw = vw + 128
    grows = rank + upr * qw
    cfg = (nsec, nz, tok, fb, vw, rank, width, cand_len)
    vmem = pl.BlockSpec(memory_space=pltpu.VMEM)
    dma = pltpu.SemaphoreType.DMA
    grad_down, grad_up = pl.pallas_call(
        functools.partial(kernel, cfg),
        out_shape=(
            jax.ShapeDtypeStruct((rank, fb), F32),
            jax.ShapeDtypeStruct((rank, vw), F32),
        ),
        in_specs=[pl.BlockSpec(memory_space=pl.ANY)]
        + [vmem] * 7
        + [pl.BlockSpec(memory_space=pltpu.SMEM)],
        out_specs=(vmem, vmem),
        scratch_shapes=[
            pltpu.VMEM((nsec, 4, r_end, fb), BF16),
            pltpu.VMEM((nsec + 1, nz, tok, slab), BF16),
            pltpu.VMEM((rows, slab), BF16),
            pltpu.VMEM((2, nz // 2, tok, pw), BF16),
            pltpu.VMEM((2 * nsec, nz, tok, pw), BF16),
            pltpu.VMEM((2 * nsec, nz, tok, pw), BF16),
            pltpu.VMEM((nsec, tok, pw), F32),
            pltpu.VMEM((4, rank, fb), F32),
            pltpu.VMEM((2, nz, 8, 128), F32),
            pltpu.VMEM((nsec, 4, grows, fb), BF16),
            pltpu.VMEM((nsec * 4, grows, fb), BF16),
            pltpu.VMEM((nz, upr * qw, fb), BF16),
            pltpu.VMEM((4, upr * qw, fb), F32),
            dma((2, 6)),
            dma((nsec, 6)),
            dma((4, 6)),
            dma((nsec, 4)),
            dma((nsec * 4, 4)),
            dma((nz,)),
            dma((nz,)),
            dma((2, nz)),
            dma((nz,)),
            dma((nz,)),
            dma((nz,)),
            dma((2, nz)),
            dma((2, nz)),
            dma((nsec, 8)),
            dma((nsec * 4, 2)),
            dma((2, 8)),
            dma((2, 8)),
        ],
        compiler_params=pltpu.CompilerParams(
            collective_id=0, has_side_effects=True, vmem_limit_bytes=56 * 1024 * 1024
        ),
        name="layers",
    )(
        block_hidden_input.reshape(blocks * cand_len, width),
        output_projection[0],
        value_projection[0],
        adapter_down_factor[0].T,
        adapter_up_factor[0],
        input_norm_gain,
        last_norm_gain.reshape(1, width),
        scoring_head_weight.reshape(1, width),
        cached_score_gradient.T,
    )
    return (grad_down.T[None], grad_up[None])


def solution(mesh):
    return jax.shard_map(
        per_device,
        mesh=mesh,
        in_specs=(
            P(None, "dp", None),
            P(None, "dp"),
            P("section", "dp", None),
            P("section", None, "dp"),
            P("section", "dp", None),
            P("section", None, None),
            P("section", None),
            P(),
            P(),
        ),
        out_specs=(P("section", "dp", None), P("section", None, None)),
        check_vma=False,
    )
```

```python
import functools

import jax
import jax.numpy as jnp
from jax import lax
from jax.experimental import pallas as pl
from jax.experimental.pallas import tpu as pltpu
from jax.sharding import PartitionSpec as P

ADAPTER_SCALE = 2.0
NORM_EPS = 1e-05
NX = 4
MESH = pl.DeviceIdType.MESH
F32 = jnp.float32
BF16 = jnp.bfloat16


def dot_nn(a, b):
    return lax.dot_general(a, b, (((1,), (0,)), ((), ())), preferred_element_type=F32)


def dot_nt(a, b):
    return lax.dot_general(a, b, (((1,), (1,)), ((), ())), preferred_element_type=F32)


def dot_tn(a, b):
    return lax.dot_general(a, b, (((0,), (0,)), ((), ())), preferred_element_type=F32)


def two_parts(value):
    high = value.astype(BF16)
    low = (value - high.astype(F32)).astype(BF16)
    return high, low


def kernel(
    cfg,
    h_ref,
    o_ref,
    v_ref,
    a_ref,
    b_ref,
    g_ref,
    lg_ref,
    sw_ref,
    cg_ref,
    gd_ref,
    gu_ref,
    weights,
    states,
    grad,
    part,
    arrived,
    spread,
    totals,
    down_sums,
    scal,
    grad_out,
    grad_in,
    up_z,
    up_q,
    own_send,
    relay_send,
    core_send,
    weight_recv,
    h_send,
    h_recv,
    part_send,
    part_recv,
    spread_send,
    spread_recv,
    scal_send,
    scal_recv,
    grad_send,
    grad_recv,
    up_send,
    up_recv,
):
    NSEC, NZ, TOK, FB, VW, RANK, WIDTH, CANDLEN = cfg
    NY = NSEC // 2
    SLAB = 4 * FB
    ROWS = NZ * TOK
    UPR = RANK // 4
    QW = VW // FB
    R_V, R_A, R_G, R_O = 0, VW, VW + RANK, VW + RANK + 32
    R_B = R_O + VW
    R_END = R_B + UPR * QW
    STARTS, SIZES = (0, R_O), (R_O // 2, (R_END - R_O) // 2)
    PW = VW + 128
    GROWS = RANK + UPR * QW

    sec = lax.axis_index("section")
    dp = lax.axis_index("dp")
    y, x_hi = sec // 2, sec % 2
    z, quarter = dp // 4, dp % 4
    x_lo, core = quarter // 2, quarter % 2
    x = x_hi * 2 + x_lo

    def device(xx, yy, zz, cc):
        return {"section": yy * 2 + xx // 2, "dp": zz * 4 + (xx % 2) * 2 + cc}

    def z_peer(d):
        zz = lax.rem(z + d, NZ)
        return zz, {"section": sec, "dp": zz * 4 + quarter}

    def place(xx, yy, cc):
        return yy * 2 + xx // 2, (xx % 2) * 2 + cc

    barrier = pltpu.get_barrier_semaphore()
    my_slot = sec * 4 + quarter

    def greet(slot, carry):
        @pl.when(slot != my_slot)
        def _():
            pl.semaphore_signal(
                barrier,
                inc=1,
                device_id={"section": slot // 4, "dp": z * 4 + slot % 4},
                device_id_type=MESH,
            )

        return carry

    lax.fori_loop(0, NSEC * 4, greet, 0)
    for d in range(1, NZ):
        pl.semaphore_signal(barrier, inc=1, device_id=z_peer(d)[1], device_id_type=MESH)

    g_own = g_ref[:, pl.ds(pl.multiple_of(dp * FB, FB), FB)]
    g1, g1r = g_own.astype(BF16), g_own
    g_rest = g1r - g1.astype(F32)
    g2 = g_rest.astype(BF16)
    g3 = (g_rest - g2.astype(F32)).astype(BF16)
    row_id = lax.broadcasted_iota(jnp.int32, (R_O - R_G, FB), 0)
    g_rows = jnp.where(
        row_id == 0,
        g1.astype(F32),
        jnp.where(row_id == 1, g2.astype(F32), jnp.where(row_id == 2, g3.astype(F32), 0.0)),
    ).astype(BF16)
    weights[sec, quarter, R_O:R_B] = o_ref[...]
    weights[sec, quarter, R_V:R_A] = v_ref[...].T
    weights[sec, quarter, R_A:R_G] = a_ref[...]
    up_rows = b_ref[pl.ds(pl.multiple_of(quarter * UPR, UPR), UPR), :]
    for w in range(QW):
        weights[sec, quarter, R_B + w * UPR : R_B + (w + 1) * UPR] = up_rows[
            :, w * FB : (w + 1) * FB
        ]
    weights[sec, quarter, R_G:R_O] = g_rows

    pl.semaphore_wait(barrier, NSEC * 4 - 1 + NZ - 1)

    def rows_half(pt, half):
        return pl.ds(pl.multiple_of(STARTS[pt] + half * SIZES[pt], 16), SIZES[pt])

    def weight_copy(xx, yy, pt, half, target, send_sem):
        k, q = place(xx, yy, core)
        return pltpu.make_async_remote_copy(
            src_ref=weights.at[k, q, rows_half(pt, half)],
            dst_ref=weights.at[k, q, rows_half(pt, half)],
            send_sem=send_sem,
            recv_sem=weight_recv.at[k * 4 + q, pt * 2 + half],
            device_id=target,
            device_id_type=MESH,
        )

    tok_row = pl.multiple_of(sec * TOK, TOK)
    HALF = NZ // 2
    SR = HALF * TOK
    stream, owner = z % 2, z // 2
    my_rows = stream * HALF + owner

    def slot_of(zz):
        return (zz % 2) * HALF + zz // 2

    sends = []
    own_states = pltpu.make_async_copy(
        h_ref.at[pl.ds(tok_row, TOK), pl.ds(pl.multiple_of(z * SLAB, SLAB), SLAB)],
        states.at[0, my_rows],
        h_send.at[0],
    )
    own_states.start()
    for d in range(1, NZ):
        zz, target = z_peer(d)
        copy = pltpu.make_async_remote_copy(
            src_ref=h_ref.at[pl.ds(tok_row, TOK), pl.ds(pl.multiple_of(zz * SLAB, SLAB), SLAB)],
            dst_ref=states.at[0, my_rows],
            send_sem=h_send.at[d],
            recv_sem=h_recv.at[z],
            device_id=target,
            device_id_type=MESH,
        )
        copy.start()
        sends.append(copy)

    def weight_wait(k, q, pt, half):
        ref = weights.at[k, q, rows_half(pt, half)]
        pltpu.make_async_copy(ref, ref, weight_recv.at[k * 4 + q, pt * 2 + half]).wait()

    def after(i, n):
        return lax.rem(i + 1, n)

    def before(i, n):
        return lax.rem(i + n - 1, n)

    y_next, y_prev, x_next, x_prev = after(y, NY), before(y, NY), after(x, NX), before(x, NX)

    def column_copies(pt):
        up, down = device(x, y_next, z, core), device(x, y_prev, z, core)
        return [
            weight_copy(x, y, pt, half, target, own_send.at[pt, i])
            for i, (half, target) in enumerate(((0, up), (1, down), (1, up), (0, down)))
        ]

    def column_relay(pt, half):
        source, target = (y_prev, y_next) if half == 0 else (y_next, y_prev)
        target = device(x, target, z, core)
        return weight_copy(x, source, pt, half, target, own_send.at[pt, 4 + half])

    def row_copies(ys, pt):
        right, left = device(x_next, y, z, core), device(x_prev, y, z, core)
        return [
            weight_copy(x, ys, pt, half, target, relay_send.at[ys * 2 + pt, i])
            for i, (half, target) in enumerate(((0, right), (1, left), (1, right), (0, left)))
        ]

    def row_relay_copy(ys, pt, half):
        source, target = (x_prev, x_next) if half == 0 else (x_next, x_prev)
        target = device(target, y, z, core)
        return weight_copy(source, ys, pt, half, target, relay_send.at[ys * 2 + pt, 4 + half])

    def row_send(ys, pt):
        for copy in row_copies(ys, pt):
            copy.start()

    def column(ys, pt):
        k, q = place(x, ys, core)
        first = jnp.where(y_next == ys, 1, 0)

        @pl.when(y != ys)
        def _():
            weight_wait(k, q, pt, first)

            @pl.when(y_prev == ys)
            def _():
                column_relay(pt, 0).start()

            @pl.when(y_next == ys)
            def _():
                column_relay(pt, 1).start()

            weight_wait(k, q, pt, 1 - first)

    def row_relay(ys, pt):
        for half, source in ((0, x_prev), (1, x_next)):
            k, q = place(source, ys, core)
            weight_wait(k, q, pt, half)
            row_relay_copy(ys, pt, half).start()

    def core_copy(layer, lo, pt):
        q = lo * 2 + core
        rows = pl.ds(STARTS[pt], 2 * SIZES[pt])
        return pltpu.make_async_remote_copy(
            src_ref=weights.at[layer, q, rows],
            dst_ref=weights.at[layer, q, rows],
            send_sem=core_send.at[layer, lo * 2 + pt],
            recv_sem=weight_recv.at[layer * 4 + q, pt * 2],
            device_id=device(x, y, z, 1 - core),
            device_id_type=MESH,
        )

    def pass_on(layer, pt):
        for lo in (0, 1):
            xs = (layer % 2) * 2 + lo
            q = lo * 2 + core

            @pl.when(jnp.logical_and(xs != x, xs != x_prev))
            def _():
                weight_wait(layer, q, pt, 0)

            @pl.when(jnp.logical_and(xs != x, xs != x_next))
            def _():
                weight_wait(layer, q, pt, 1)

            core_copy(layer, lo, pt).start()

    def take_over(layer, pt):
        for lo in (0, 1):
            q = lo * 2 + (1 - core)
            ref = weights.at[layer, q, pl.ds(STARTS[pt], 2 * SIZES[pt])]
            pltpu.make_async_copy(ref, ref, weight_recv.at[layer * 4 + q, pt * 2]).wait()

    @pl.when(jnp.logical_and(y == 0, NY > 1))
    def _():
        for copy in column_copies(0) + column_copies(1):
            copy.start()

    for pt in (0, 1):
        column(0, pt)
        row_send(0, pt)

    @pl.when(y != 0)
    def _():
        for copy in column_copies(0) + column_copies(1):
            copy.start()

    row_relay(0, 0)

    def gains(layer, q):
        return jnp.sum(weights[layer, q, R_G : R_G + 16].astype(F32), axis=0, keepdims=True)

    def ups(layer):
        return [
            jnp.concatenate(
                [weights[layer, q, R_B + w * UPR : R_B + (w + 1) * UPR] for q in range(4)], axis=0
            )
            for w in range(QW)
        ]

    def peer(st, d):
        zz = 2 * lax.rem(owner + d, HALF) + st
        return zz, {"section": sec, "dp": zz * 4 + quarter}

    def part_copy(st, step, d, lanes):
        zz, target = peer(st, d)
        return pltpu.make_async_remote_copy(
            src_ref=part.at[st, zz // 2, :, pl.ds(0, lanes)],
            dst_ref=arrived.at[step, z, :, pl.ds(0, lanes)],
            send_sem=part_send.at[st, d],
            recv_sem=part_recv.at[z],
            device_id=target,
            device_id_type=MESH,
        )

    def spread_copy(step, d, lanes):
        target = z_peer(d)[1]
        return pltpu.make_async_remote_copy(
            src_ref=spread.at[step, my_rows, :, pl.ds(0, lanes)],
            dst_ref=spread.at[step, my_rows, :, pl.ds(0, lanes)],
            send_sem=spread_send.at[d],
            recv_sem=spread_recv.at[z],
            device_id=target,
            device_id_type=MESH,
        )

    far_first = sorted(range(1, NZ), key=lambda d: -min(d, NZ - d))
    owners_far_first = sorted(range(1, HALF), key=lambda d: -min(d, HALF - d))

    def exchange_start(st, step, lanes):
        for d in owners_far_first:
            part_copy(st, step, d, lanes).start()

        @pl.when(stream != st)
        def _():
            part_copy(st, step, 0, lanes).start()

    def exchange_sum(st, step, lanes):
        for d in range(1, NZ):
            zz = lax.rem(z + d, NZ)
            ref = arrived.at[step, zz, :, pl.ds(0, lanes)]
            pltpu.make_async_copy(ref, ref, part_recv.at[zz]).wait()
        total = part[st, owner, :, 0:lanes].astype(F32)
        for d in range(1, NZ):
            total = total + arrived[step, lax.rem(z + d, NZ), :, 0:lanes].astype(F32)
        return total

    def spread_start(step, lanes):
        for d in far_first:
            spread_copy(step, d, lanes).start()

    def exchange_end(st, step, part_lanes, lanes):
        @pl.when(stream != st)
        def _():
            part_copy(st, step, 0, part_lanes).wait_send()

        for d in range(1, HALF):
            part_copy(st, step, d, part_lanes).wait_send()

        def arrive(d):
            zz = peer(st, d)[0]
            ref = spread.at[step, slot_of(zz), :, pl.ds(0, lanes)]
            pltpu.make_async_copy(ref, ref, spread_recv.at[zz]).wait()

        @pl.when(stream != st)
        def _():
            arrive(0)

        for d in range(1, HALF):
            arrive(d)

        @pl.when(stream == st)
        def _():
            for d in range(1, NZ):
                spread_copy(step, d, lanes).wait_send()

    lane_stream = lax.broadcasted_iota(jnp.int32, (SR, 128), 1)
    lane_own = lax.broadcasted_iota(jnp.int32, (TOK, 128), 1)

    def put_scalar(rank_part, scalar, lanes):
        high, low = two_parts(scalar)
        padded = jnp.concatenate([rank_part, jnp.zeros_like(rank_part)], axis=1)
        return jnp.where(
            lanes == RANK,
            high.astype(F32),
            jnp.where(lanes == RANK + 1, low.astype(F32), padded),
        )

    def get_scalar(tile, lanes):
        return jnp.sum(jnp.where(lanes >= RANK, tile, 0.0), axis=1, keepdims=True)

    pass_on(jnp.int32(0), 0)
    own_states.wait()
    for d in range(1, NZ):
        zz = lax.rem(z + d, NZ)
        ref = states.at[0, slot_of(zz)]
        pltpu.make_async_copy(ref, ref, h_recv.at[zz]).wait()

    def rows_of(layer, st, q):
        own_rows = slice(st * HALF, (st + 1) * HALF)
        return states[layer, own_rows, :, q * FB : (q + 1) * FB].reshape(SR, FB)

    def forward_part(st, layer):
        ss = jnp.zeros((SR, 1), F32)
        value = jnp.zeros((SR, VW + RANK), F32)
        for q in range(4):
            xq = rows_of(layer, st, q).astype(F32)
            ss = ss + jnp.sum(xq * xq, axis=1, keepdims=True)
            xg = (xq * gains(layer, q)).astype(BF16)
            value = value + dot_nt(xg, weights[layer, q, R_V:R_G])
        part[st, :, :, 0:VW] = value[:, 0:VW].astype(BF16).reshape(HALF, TOK, VW)
        part[st, :, :, VW:PW] = (
            put_scalar(value[:, VW:], ss, lane_stream).astype(BF16).reshape(HALF, TOK, 128)
        )
        exchange_start(st, layer, PW)

    def forward_own(st, layer):
        @pl.when(stream == st)
        def _():
            up_factor = ups(layer)
            total = exchange_sum(st, layer, PW)
            totals[layer] = total
            tail = total[:, VW:PW]
            r = lax.rsqrt(get_scalar(tail, lane_own) / WIDTH + NORM_EPS)
            t = (r * tail[:, 0:RANK]).astype(BF16)
            for w, up in enumerate(up_factor):
                cols = slice(w * FB, (w + 1) * FB)
                spread[layer, my_rows, :, cols] = (
                    r * total[:, cols] + ADAPTER_SCALE * dot_nn(t, up)
                ).astype(BF16)
            spread_start(layer, VW)

    def forward_end(st, layer):
        exchange_end(st, layer, PW, VW)
        own_rows = slice(st * HALF, (st + 1) * HALF)
        v = spread[layer, own_rows, :, 0:VW].reshape(SR, VW)
        for q in range(4):
            xq = rows_of(layer, st, q).astype(F32)
            states[layer + 1, own_rows, :, q * FB : (q + 1) * FB] = (
                (xq + dot_nn(v, weights[layer, q, R_O:R_B])).astype(BF16).reshape(HALF, TOK, FB)
            )

    take_over(jnp.int32(0), 0)
    forward_part(0, jnp.int32(0))
    row_relay(0, 1)
    for pt in (0, 1):
        for ys in range(1, NY):
            column(ys, pt)
            if ys == 1:
                row_send(ys, pt)

    def forward_step(layer, carry):
        @pl.when(layer > 0)
        def _():
            forward_end(1, layer - 1)

        forward_part(1, layer)

        pass_on(layer, 1)

        @pl.when(jnp.logical_and(layer % 2 == 1, (layer + 1) // 2 < NY))
        def _():
            row_relay((layer + 1) // 2, 1)

        @pl.when(jnp.logical_and(layer % 2 == 1, (layer + 3) // 2 < NY))
        def _():
            for pt in (0, 1):
                row_send((layer + 3) // 2, pt)

        take_over(layer, 1)
        forward_own(0, layer)
        forward_own(1, layer)

        @pl.when(jnp.logical_and(layer % 2 == 0, layer // 2 + 1 < NY))
        def _():
            row_relay(layer // 2 + 1, 0)

        @pl.when(layer + 1 < NSEC)
        def _():
            pass_on(layer + 1, 0)

        forward_end(0, layer)

        @pl.when(layer + 1 < NSEC)
        def _():
            take_over(layer + 1, 0)
            forward_part(0, layer + 1)

        return carry

    slab = pl.ds(pl.multiple_of(z * SLAB, SLAB), SLAB)

    def scal_copy(st, d):
        return pltpu.make_async_remote_copy(
            src_ref=scal.at[st, z],
            dst_ref=scal.at[st, z],
            send_sem=scal_send.at[st, d],
            recv_sem=scal_recv.at[st, z],
            device_id=z_peer(d)[1],
            device_id_type=MESH,
        )

    def last_rows(st):
        rows = states[NSEC, st * HALF : (st + 1) * HALF]
        return rows.reshape(SR, SLAB).astype(F32), lg_ref[:, slab] * sw_ref[:, slab]

    def seed_start(st):
        last, head = last_rows(st)
        ss = jnp.sum(last * last, axis=1, keepdims=True)
        inner = jnp.sum(last * head, axis=1, keepdims=True)
        rows = lax.broadcasted_iota(jnp.int32, (SR, 128), 0)
        mine = jnp.logical_and(
            stream == st, jnp.logical_and(rows >= owner * TOK, rows < (owner + 1) * TOK)
        )
        token_grad = jnp.where(mine, cg_ref[0, sec * TOK // CANDLEN], 0.0)
        table = jnp.where(
            lane_stream == 0,
            ss,
            jnp.where(lane_stream == 1, inner, jnp.where(lane_stream == 2, token_grad, 0.0)),
        )
        scal[st, z] = jnp.concatenate([table] * (128 // SR), axis=0).T[0:8]
        for d in far_first:
            copy = scal_copy(st, d)
            copy.start()
            sends.append(copy)

    def seed_end(st):
        for d in range(1, NZ):
            zz = lax.rem(z + d, NZ)
            ref = scal.at[st, zz]
            pltpu.make_async_copy(ref, ref, scal_recv.at[st, zz]).wait()
        table = jnp.concatenate([jnp.sum(scal[st], axis=0)] * 16, axis=0).T[0:SR]
        ss, inner, token_grad = (
            jnp.sum(jnp.where(lane_stream == i, table, 0.0), axis=1, keepdims=True)
            for i in range(3)
        )
        last, head = last_rows(st)
        factor = lax.rsqrt(ss / WIDTH + NORM_EPS)
        token_grad = token_grad / CANDLEN
        grad[st * SR : (st + 1) * SR] = (
            token_grad * factor * head
            - token_grad * factor * factor * factor * inner / WIDTH * last
        ).astype(BF16)

    lax.fori_loop(0, NSEC, forward_step, 0)
    seed_start(0)
    forward_end(1, jnp.int32(NSEC - 1))
    seed_start(1)
    seed_end(0)

    grad_rows = (pl.ds(0, RANK), pl.ds(RANK, GROWS - RANK))

    def grad_copy(layer, q, pt):
        return pltpu.make_async_remote_copy(
            src_ref=grad_out.at[layer, q, grad_rows[pt]],
            dst_ref=grad_in.at[my_slot, grad_rows[pt]],
            send_sem=grad_send.at[layer, q * 2 + pt],
            recv_sem=grad_recv.at[my_slot, pt],
            device_id={"section": layer, "dp": z * 4 + q},
            device_id_type=MESH,
        )

    def grad_leave(layer, q, pt):
        here = jnp.logical_and(layer == sec, quarter == q)

        @pl.when(jnp.logical_not(here))
        def _():
            grad_copy(layer, q, pt).start()

        @pl.when(here)
        def _():
            grad_in[my_slot, grad_rows[pt]] = grad_out[layer, q, grad_rows[pt]]

    def backward_part(st, layer):
        value = jnp.zeros((SR, VW), F32)
        for q in range(4):
            value = value + dot_nt(
                grad[st * SR : (st + 1) * SR, q * FB : (q + 1) * FB], weights[layer, q, R_O:R_B]
            )
        part[st, :, :, 0:VW] = value.astype(BF16).reshape(HALF, TOK, VW)
        exchange_start(st, 2 * NSEC - 1 - layer, VW)

    def backward_own(st, layer):
        step = 2 * NSEC - 1 - layer

        @pl.when(stream == st)
        def _():
            forward_total = totals[layer]
            tail = forward_total[:, VW:PW]
            r = lax.rsqrt(get_scalar(tail, lane_own) / WIDTH + NORM_EPS)
            t = (r * tail[:, 0:RANK]).astype(BF16)
            up_factor = ups(layer)
            dv = exchange_sum(st, step, VW).astype(BF16)
            dt32 = jnp.zeros((TOK, RANK), F32)
            for w, up in enumerate(up_factor):
                dt32 = dt32 + dot_nt(dv[:, w * FB : (w + 1) * FB], up)
            dt = (ADAPTER_SCALE * dt32).astype(BF16)
            dvf, dtf = dv.astype(F32), dt.astype(F32)
            inner = jnp.sum(dvf * forward_total[:, 0:VW], axis=1, keepdims=True) + jnp.sum(
                dtf * tail[:, 0:RANK], axis=1, keepdims=True
            )
            shrink = r * r * r * inner / WIDTH
            spread[step, my_rows, :, 0:VW] = (r * dvf).astype(BF16)
            spread[step, my_rows, :, VW:PW] = put_scalar(r * dtf, shrink, lane_own).astype(BF16)
            spread_start(step, PW)
            up_sum = (ADAPTER_SCALE * dot_tn(t, dv)).astype(BF16)
            for q in range(4):
                for w in range(QW):
                    grad_out[layer, q, RANK + w * UPR : RANK + (w + 1) * UPR] = up_sum[
                        q * UPR : (q + 1) * UPR, w * FB : (w + 1) * FB
                    ]
                grad_leave(layer, q, 1)

    def backward_end(st, layer):
        step = 2 * NSEC - 1 - layer
        exchange_end(st, step, VW, PW)
        both = spread[step, st * HALF : (st + 1) * HALF].reshape(SR, PW)
        scaled = both[:, 0 : VW + RANK]
        shrink = get_scalar(both[:, VW:PW].astype(F32), lane_stream)
        own_rows = slice(st * SR, (st + 1) * SR)

        @pl.when(layer > 0)
        def _():
            for q in range(4):
                cols = slice(q * FB, (q + 1) * FB)
                du = dot_nn(scaled, weights[layer, q, R_V:R_G])
                grad[own_rows, cols] = (
                    grad[own_rows, cols].astype(F32)
                    + du * gains(layer, q)
                    - shrink * rows_of(layer, st, q).astype(F32)
                ).astype(BF16)

    def backward_sums(st, layer):
        step = 2 * NSEC - 1 - layer
        rdt = spread[step, st * HALF : (st + 1) * HALF, :, VW : VW + RANK].reshape(SR, RANK)
        for q in range(4):
            share = dot_tn(rdt, rows_of(layer, st, q)) * gains(layer, q)
            if st == 0:
                down_sums[q] = share
                continue
            grad_out[layer, q, 0:RANK] = (down_sums[q] + share).astype(BF16)
            grad_leave(layer, q, 0)

    backward_part(0, jnp.int32(NSEC - 1))
    seed_end(1)

    def backward_step(index, carry):
        layer = NSEC - 1 - index

        @pl.when(index > 0)
        def _():
            backward_end(1, layer + 1)

        backward_part(1, layer)

        @pl.when(index > 0)
        def _():
            backward_sums(1, layer + 1)

        backward_own(0, layer)
        backward_own(1, layer)
        backward_end(0, layer)

        @pl.when(layer > 0)
        def _():
            backward_part(0, layer - 1)

        backward_sums(0, layer)
        return carry

    lax.fori_loop(0, NSEC, backward_step, 0)
    backward_end(1, jnp.int32(0))
    backward_sums(1, jnp.int32(0))

    def collect(pt):
        def wait_slot(slot, carry):
            @pl.when(slot != my_slot)
            def _():
                ref = grad_in.at[slot, grad_rows[pt]]
                pltpu.make_async_copy(ref, ref, grad_recv.at[slot, pt]).wait()

            return carry

        lax.fori_loop(0, NSEC * 4, wait_slot, 0)
        return jnp.sum(grad_in[:, grad_rows[pt]].astype(F32), axis=0)

    up_z[z] = collect(1).astype(BF16)
    for d in far_first:
        zz, target = z_peer(d)
        copy = pltpu.make_async_remote_copy(
            src_ref=up_z.at[z],
            dst_ref=up_z.at[z],
            send_sem=up_send.at[0, d],
            recv_sem=up_recv.at[0, z],
            device_id=target,
            device_id_type=MESH,
        )
        copy.start()
        sends.append(copy)
    for d in range(1, NZ):
        zz = lax.rem(z + d, NZ)
        pltpu.make_async_copy(up_z.at[zz], up_z.at[zz], up_recv.at[0, zz]).wait()
    up_q[quarter] = jnp.sum(up_z[...].astype(F32), axis=0)
    for d in range(1, 4):
        copy = pltpu.make_async_remote_copy(
            src_ref=up_q.at[quarter],
            dst_ref=up_q.at[quarter],
            send_sem=up_send.at[1, d],
            recv_sem=up_recv.at[1, quarter],
            device_id={"section": sec, "dp": z * 4 + lax.rem(quarter + d, 4)},
            device_id_type=MESH,
        )
        copy.start()
        sends.append(copy)
    gd_ref[...] = collect(0)
    for d in range(1, 4):
        qq = lax.rem(quarter + d, 4)
        pltpu.make_async_copy(up_q.at[qq], up_q.at[qq], up_recv.at[1, qq]).wait()
    for q in range(4):
        for w in range(QW):
            gu_ref[q * UPR : (q + 1) * UPR, w * FB : (w + 1) * FB] = up_q[
                q, w * UPR : (w + 1) * UPR
            ]

    for copy in sends:
        copy.wait_send()
    for pt in (0, 1):
        if NY > 1:
            for copy in column_copies(pt) + [column_relay(pt, 0), column_relay(pt, 1)]:
                copy.wait_send()
        for ys in range(NY):
            for copy in row_copies(ys, pt) + [row_relay_copy(ys, pt, half) for half in (0, 1)]:
                copy.wait_send()

    def drain(layer, carry):
        for lo in (0, 1):
            for pt in (0, 1):
                core_copy(layer, lo, pt).wait_send()
        for q in range(4):

            @pl.when(jnp.logical_not(jnp.logical_and(layer == sec, quarter == q)))
            def _():
                for pt in (0, 1):
                    grad_copy(layer, q, pt).wait_send()

        return carry

    lax.fori_loop(0, NSEC, drain, 0)


def per_device(
    block_hidden_input,
    cached_score_gradient,
    value_projection,
    output_projection,
    adapter_down_factor,
    adapter_up_factor,
    input_norm_gain,
    last_norm_gain,
    scoring_head_weight,
):
    nsec = lax.axis_size("section")
    nz = lax.axis_size("dp") // 4
    blocks, cand_len, width = block_hidden_input.shape
    tok = blocks * cand_len // nsec
    fb, vw = value_projection.shape[1:]
    rank = adapter_down_factor.shape[2]
    slab, rows = 4 * fb, nz * tok
    upr, qw = rank // 4, vw // fb
    r_end = 2 * vw + rank + upr * qw + 32
    pw = vw + 128
    grows = rank + upr * qw
    cfg = (nsec, nz, tok, fb, vw, rank, width, cand_len)
    vmem = pl.BlockSpec(memory_space=pltpu.VMEM)
    dma = pltpu.SemaphoreType.DMA
    grad_down, grad_up = pl.pallas_call(
        functools.partial(kernel, cfg),
        out_shape=(
            jax.ShapeDtypeStruct((rank, fb), F32),
            jax.ShapeDtypeStruct((rank, vw), F32),
        ),
        in_specs=[pl.BlockSpec(memory_space=pl.ANY)]
        + [vmem] * 7
        + [pl.BlockSpec(memory_space=pltpu.SMEM)],
        out_specs=(vmem, vmem),
        scratch_shapes=[
            pltpu.VMEM((nsec, 4, r_end, fb), BF16),
            pltpu.VMEM((nsec + 1, nz, tok, slab), BF16),
            pltpu.VMEM((rows, slab), BF16),
            pltpu.VMEM((2, nz // 2, tok, pw), BF16),
            pltpu.VMEM((2 * nsec, nz, tok, pw), BF16),
            pltpu.VMEM((2 * nsec, nz, tok, pw), BF16),
            pltpu.VMEM((nsec, tok, pw), F32),
            pltpu.VMEM((4, rank, fb), F32),
            pltpu.VMEM((2, nz, 8, 128), F32),
            pltpu.VMEM((nsec, 4, grows, fb), BF16),
            pltpu.VMEM((nsec * 4, grows, fb), BF16),
            pltpu.VMEM((nz, upr * qw, fb), BF16),
            pltpu.VMEM((4, upr * qw, fb), F32),
            dma((2, 6)),
            dma((nsec, 6)),
            dma((nsec, 4)),
            dma((nsec * 4, 4)),
            dma((nz,)),
            dma((nz,)),
            dma((2, nz)),
            dma((nz,)),
            dma((nz,)),
            dma((nz,)),
            dma((2, nz)),
            dma((2, nz)),
            dma((nsec, 8)),
            dma((nsec * 4, 2)),
            dma((2, 8)),
            dma((2, 8)),
        ],
        compiler_params=pltpu.CompilerParams(
            collective_id=0, has_side_effects=True, vmem_limit_bytes=56 * 1024 * 1024
        ),
        name="layers",
    )(
        block_hidden_input.reshape(blocks * cand_len, width),
        output_projection[0],
        value_projection[0],
        adapter_down_factor[0].T,
        adapter_up_factor[0],
        input_norm_gain,
        last_norm_gain.reshape(1, width),
        scoring_head_weight.reshape(1, width),
        cached_score_gradient.T,
    )
    return (grad_down.T[None], grad_up[None])


def solution(mesh):
    return jax.shard_map(
        per_device,
        mesh=mesh,
        in_specs=(
            P(None, "dp", None),
            P(None, "dp"),
            P("section", "dp", None),
            P("section", None, "dp"),
            P("section", "dp", None),
            P("section", None, None),
            P("section", None),
            P(),
            P(),
        ),
        out_specs=(P("section", "dp", None), P("section", None, None)),
        check_vma=False,
    )
```
